512 devices in a mesh: dom: 64 (over z, x, core), feat: 8 (over y).
Axes of the slice: x: 4, y: 8, z: 8, core: 2. Of those that a mesh axis runs over, the one named last changes fastest.
Arguments:
- node_in: bfloat16 [40960, 512], P('dom'), may hold values from -6 to 6
- local_edges: bfloat16 [65536, 512], P(('dom', 'feat')), may hold values from -6 to 6
- cut_edges: bfloat16 [524288, 512], P(('dom', 'feat')), may hold values from -6 to 6
- node_cot: bfloat16 [40960, 512], P(('dom', 'feat')), may hold values from -6 to 6
- edge_w1: bfloat16 [1536, 512], P('feat'), may hold values from -0.15625 to 0.15625
- edge_w2: bfloat16 [512, 512], P('feat'), may hold values from -0.25 to 0.25
- node_w1: bfloat16 [1024, 512], P('feat'), may hold values from -0.1875 to 0.1875
- node_w2: bfloat16 [512, 512], P('feat'), may hold values from -0.25 to 0.25
- edge_b1: float32 [512], replicated, may hold values from -3 to 3
- edge_b2: float32 [512], replicated, may hold values from -3 to 3
- edge_gain: float32 [512], replicated, may hold values from 0.5 to 1.5
- edge_shift: float32 [512], replicated, may hold values from -3 to 3
- node_b1: float32 [512], replicated, may hold values from -3 to 3
- node_b2: float32 [512], replicated, may hold values from -3 to 3
- node_gain: float32 [512], replicated, may hold values from 0.5 to 1.5
- node_shift: float32 [512], replicated, may hold values from -3 to 3
- local_send: int32 [65536], P(('dom', 'feat')), may hold values from 0 to 639
- local_recv: int32 [65536], P(('dom', 'feat')), may hold values from 0 to 79
- cut_send: int32 [64, 8, 1024], P('dom', 'feat'), may hold values from 0 to 15
- cut_recv: int32 [64, 8, 1024], P('dom', 'feat'), may hold values from 0 to 79
- cut_count: int32 [64, 8, 64], P('dom', 'feat'), may hold values from 0 to 16, as said below
Outputs:
- node_out: bfloat16 [40960, 512], P(('dom', 'feat'))
- node_grad: float32 [40960, 512], P(('dom', 'feat'))
- local_grad: bfloat16 [65536, 512], P(('dom', 'feat'))
- cut_grad: bfloat16 [524288, 512], P(('dom', 'feat'))
The draws below stay inside these ranges and needn't reach their ends.
Inputs may be any that keep to these rules, and one draw needn't show every extreme that they name: `cut_count`: every device has one source partition whose 16 slots are all live, and at least one device has all its slots live.
All inputs are finite; a program needn't handle non-finite values.
Results may differ from the reference program's by a relative error of at most 0.02.
Values may be sent and summed in bfloat16 or wider, within the bound.
No kernel may reach another device: no remote copies, remote signals or barrier semaphores. Data moves between devices by JAX's collectives and lax.ppermute only.
A program may use at most 64 MiB of HBM per device.

```python
import jax
import jax.numpy as jnp
from jax import lax

D = 512
H = 512
NODE_DEV = 80
LOC_DEV = 128
BORDER = 16
SLOT_DEV = 16
PART = 640
NODES = 40960
EDGES_LOC = 65536
EDGES_CUT = 524288
N_DOM = 64
N_FEAT = 8


def draw_cut_count(key, part):
    key = jax.random.fold_in(key, 7)
    subkeys = jax.random.split(key, 5)
    block_shape = (N_DOM, N_FEAT, N_DOM)
    heavy_source = jax.random.randint(subkeys[0], (1, 1, N_DOM), 1, 5)
    base_count = jax.random.randint(subkeys[1], block_shape, 0, SLOT_DEV + 1)
    counts = base_count * heavy_source // 4
    full_source = jax.random.randint(subkeys[2], (N_DOM, N_FEAT, 1), 0, N_DOM)
    source_pos = lax.broadcasted_iota(jnp.int32, block_shape, 2)
    counts = jnp.where(source_pos == full_source, SLOT_DEV, counts)
    busy_dom = jax.random.randint(subkeys[3], (), 0, N_DOM)
    busy_feat = jax.random.randint(subkeys[4], (), 0, N_FEAT)
    dom_pos = lax.broadcasted_iota(jnp.int32, block_shape, 0)
    feat_pos = lax.broadcasted_iota(jnp.int32, block_shape, 1)
    busiest = jnp.logical_and(dom_pos == busy_dom, feat_pos == busy_feat)
    return jnp.where(busiest, SLOT_DEV, counts).astype(jnp.int32)


def set_ends(array, key, least, high):
    shape = array.shape
    spot = [jax.random.randint(jax.random.fold_in(key, axis), (), 0, shape[axis]) for axis in range(len(shape))]
    array = array.at[tuple(spot)].set(least)
    longest = shape.index(max(shape))
    spot[longest] = (spot[longest] + 1) % shape[longest]
    return array.at[tuple(spot)].set(high)


def levels(rng, dims, pieces, smallest, top_value):
    def one(position, parts):
        heights = jax.random.uniform(jax.random.fold_in(jax.random.fold_in(rng, 6), position), (parts,), jnp.float32, smallest / len(pieces), top_value / len(pieces))
        return jnp.repeat(jnp.exp(heights), dims[position] // parts).reshape((-1,) + (1,) * (len(dims) - position - 1))

    level = one(*pieces[0])
    for cut in pieces[1:]:
        level = level * one(*cut)
    return level


def scatter_about(key, shape, deviation, bound, shards=(), kind=jnp.bfloat16):
    result = deviation * jax.random.normal(key, shape, jnp.float32)
    if shards:
        result = result * levels(key, shape, shards, -0.22, 0.18)
    return jnp.clip(result, -bound, bound).astype(kind)


def setup_inputs(seed: int = 0) -> dict:
    key_list = jax.random.split(jax.random.key(seed), 22)
    node_in = scatter_about(key_list[0], (NODES, D), 1.0, 6.0, ((0, 64),))
    local_edges = scatter_about(key_list[1], (EDGES_LOC, D), 1.0, 6.0, ((0, 512),))
    cut_edges = scatter_about(key_list[2], (EDGES_CUT, D), 1.0, 6.0, ((0, 512),))
    node_cot = scatter_about(key_list[3], (NODES, D), 1.0, 6.0, ((0, 512),))
    edge_w1 = scatter_about(key_list[4], (3 * D, H), (3 * D) ** -0.5, 0.15625, ((0, 8),))
    edge_w2 = scatter_about(key_list[5], (H, D), H ** -0.5, 0.25, ((0, 8),))
    node_w1 = scatter_about(key_list[6], (2 * D, H), (2 * D) ** -0.5, 0.1875, ((0, 8),))
    node_w2 = scatter_about(key_list[7], (H, D), H ** -0.5, 0.25, ((0, 8),))
    edge_b1 = scatter_about(key_list[8], (H,), 0.5, 3.0, (), jnp.float32)
    edge_b2 = scatter_about(key_list[9], (D,), 0.5, 3.0, (), jnp.float32)
    edge_gain = jnp.clip(1.0 + 0.1 * jax.random.normal(key_list[10], (D,), jnp.float32), 0.5, 1.5)
    edge_shift = scatter_about(key_list[11], (D,), 0.5, 3.0, (), jnp.float32)
    node_b1 = scatter_about(key_list[12], (H,), 0.5, 3.0, (), jnp.float32)
    node_b2 = scatter_about(key_list[13], (D,), 0.5, 3.0, (), jnp.float32)
    node_gain = jnp.clip(1.0 + 0.1 * jax.random.normal(key_list[14], (D,), jnp.float32), 0.5, 1.5)
    node_shift = scatter_about(key_list[15], (D,), 0.5, 3.0, (), jnp.float32)
    local_send = set_ends(jax.random.randint(key_list[16], (EDGES_LOC,), 0, PART), jax.random.fold_in(key_list[16], 1), 0, PART - 1).astype(jnp.int32)
    local_recv = set_ends(jax.random.randint(key_list[17], (EDGES_LOC,), 0, NODE_DEV), jax.random.fold_in(key_list[17], 1), 0, NODE_DEV - 1).astype(jnp.int32)
    cut_send = set_ends(jax.random.randint(key_list[18], (N_DOM, N_FEAT, N_DOM * SLOT_DEV), 0, BORDER), jax.random.fold_in(key_list[18], 1), 0, BORDER - 1).astype(jnp.int32)
    cut_recv = set_ends(jax.random.randint(key_list[19], (N_DOM, N_FEAT, N_DOM * SLOT_DEV), 0, NODE_DEV), jax.random.fold_in(key_list[19], 1), 0, NODE_DEV - 1).astype(jnp.int32)
    cut_count = draw_cut_count(jax.random.fold_in(key_list[21], 71), 0)
    return dict(node_in=node_in, local_edges=local_edges, cut_edges=cut_edges, node_cot=node_cot, edge_w1=edge_w1, edge_w2=edge_w2, node_w1=node_w1, node_w2=node_w2, edge_b1=edge_b1, edge_b2=edge_b2, edge_gain=edge_gain, edge_shift=edge_shift, node_b1=node_b1, node_b2=node_b2, node_gain=node_gain, node_shift=node_shift, local_send=local_send, local_recv=local_recv, cut_send=cut_send, cut_recv=cut_recv, cut_count=cut_count)


NORM_EPS = 1e-05

def normalize(values):
    centered = values - lax.optimization_barrier(jnp.mean(values, axis=-1, keepdims=True))
    inv_std = lax.rsqrt(lax.optimization_barrier(jnp.mean(centered * centered, axis=-1, keepdims=True)) + NORM_EPS)
    return (centered * inv_std, inv_std)

def norm_back(grad_out, normed, inv_std, norm_gain):
    scaled = grad_out * norm_gain
    first_mean = lax.optimization_barrier(jnp.mean(scaled, axis=-1, keepdims=True))
    second_mean = lax.optimization_barrier(jnp.mean(scaled * normed, axis=-1, keepdims=True))
    return inv_std * (scaled - first_mean - normed * second_mean)

def silu_slope(pre_act):
    sigmoid_val = jax.nn.sigmoid(pre_act)
    return sigmoid_val * (1.0 + pre_act * (1.0 - sigmoid_val))

def times_transpose(operand, weight):
    return lax.dot_general(operand, weight, (((1,), (1,)), ((), ())), preferred_element_type=jnp.float32)

def edge_forward(edge_rows, senders, receivers, live_mask, params):
    w_first, w_second, b_first, b_second, norm_gain, norm_shift = params
    joined = jnp.concatenate([edge_rows, senders, receivers], axis=1)
    pre_act = jnp.dot(joined, w_first, preferred_element_type=jnp.float32) + b_first
    activation = jax.nn.silu(pre_act).astype(jnp.bfloat16)
    pre_norm = jnp.dot(activation, w_second, preferred_element_type=jnp.float32) + b_second
    normed, inv_std = normalize(pre_norm)
    message = live_mask[:, None] * (edge_rows.astype(jnp.float32) + normed * norm_gain + norm_shift)
    return (message, (pre_act, normed, inv_std))

def edge_backward(grad_message, stored, params):
    w_first, w_second, b_first, b_second, norm_gain, norm_shift = params
    pre_act, normed, inv_std = stored
    grad_norm = norm_back(grad_message, normed, inv_std, norm_gain).astype(jnp.bfloat16)
    grad_pre = (times_transpose(grad_norm, w_second) * silu_slope(pre_act)).astype(jnp.bfloat16)
    grad_in = times_transpose(grad_pre, w_first)
    feat_width = grad_message.shape[1]
    return (grad_message + grad_in[:, :feat_width], grad_in[:, feat_width:2 * feat_width], grad_in[:, 2 * feat_width:])

def reference(node_in, local_edges, cut_edges, node_cot, edge_w1, edge_w2, node_w1, node_w2, edge_b1, edge_b2, edge_gain, edge_shift, node_b1, node_b2, node_gain, node_shift, local_send, local_recv, cut_send, cut_recv, cut_count):
    feat_width = node_in.shape[1]
    part_rows = NODE_DEV * N_FEAT
    cut_rows = N_DOM * SLOT_DEV
    local_rows = N_FEAT * LOC_DEV
    edge_params = (edge_w1, edge_w2, edge_b1, edge_b2, edge_gain, edge_shift)
    node_tables = node_in.reshape(N_DOM, part_rows, feat_width)
    borders = node_tables[:, :BORDER].reshape(N_DOM * BORDER, feat_width)
    by_target = jnp.transpose(cut_send.reshape(N_DOM, N_FEAT, N_DOM, SLOT_DEV), (2, 1, 0, 3))
    source_base = (jnp.arange(N_DOM, dtype=jnp.int32) * BORDER).reshape(1, 1, N_DOM, 1)
    cut_sources = (by_target + source_base).reshape(N_DOM, N_FEAT * cut_rows)
    owner_base = (jnp.arange(N_FEAT, dtype=jnp.int32) * NODE_DEV).reshape(1, N_FEAT, 1)
    cut_targets = (cut_recv + owner_base).reshape(N_DOM, N_FEAT * cut_rows)
    slot_pos = jnp.arange(SLOT_DEV, dtype=jnp.int32).reshape(1, 1, 1, SLOT_DEV)
    cut_live = (slot_pos < cut_count[..., None]).astype(jnp.float32).reshape(N_DOM, N_FEAT * cut_rows)
    local_targets = (local_recv.reshape(N_DOM, N_FEAT, LOC_DEV) + owner_base).reshape(N_DOM, local_rows)
    local_sources = local_send.reshape(N_DOM, local_rows)
    local_blocks = local_edges.reshape(N_DOM, local_rows, feat_width)
    cut_blocks = cut_edges.reshape(N_DOM, N_FEAT * cut_rows, feat_width)
    cot_blocks = node_cot.reshape(N_DOM, part_rows, feat_width)

    def one_partition(border_grad, inputs):
        node_table, local_block, cut_block, local_source, local_target, cut_source, cut_target, live_cut, cot_block = inputs
        edge_rows = jnp.concatenate([local_block, cut_block], axis=0)
        senders = jnp.concatenate([node_table[local_source], borders[cut_source]], axis=0)
        targets = jnp.concatenate([local_target, cut_target])
        receivers = node_table[targets]
        live_mask = jnp.concatenate([jnp.ones((local_rows,), jnp.float32), live_cut])
        message, stored = edge_forward(edge_rows, senders, receivers, live_mask, edge_params)
        aggregate = jax.ops.segment_sum(message, targets, num_segments=part_rows).astype(jnp.bfloat16)
        node_joined = jnp.concatenate([node_table, aggregate], axis=1)
        node_pre = jnp.dot(node_joined, node_w1, preferred_element_type=jnp.float32) + node_b1
        node_act = jax.nn.silu(node_pre).astype(jnp.bfloat16)
        node_norm_in = jnp.dot(node_act, node_w2, preferred_element_type=jnp.float32) + node_b2
        node_normed, node_inv = normalize(node_norm_in)
        node_out = (node_table.astype(jnp.float32) + node_normed * node_gain + node_shift).astype(jnp.bfloat16)
        cotangent = cot_block.astype(jnp.float32)
        grad_node_norm = norm_back(cotangent, node_normed, node_inv, node_gain).astype(jnp.bfloat16)
        grad_node_pre = (times_transpose(grad_node_norm, node_w2) * silu_slope(node_pre)).astype(jnp.bfloat16)
        grad_node_in = times_transpose(grad_node_pre, node_w1)
        grad_agg = grad_node_in[:, feat_width:]
        grad_message = live_mask[:, None] * grad_agg[targets]
        grad_edge, grad_send, grad_recv = edge_backward(grad_message, stored, edge_params)
        node_grad = cotangent + grad_node_in[:, :feat_width]
        node_grad = node_grad + jax.ops.segment_sum(grad_recv, targets, num_segments=part_rows)
        node_grad = node_grad + jax.ops.segment_sum(grad_send[:local_rows], local_source, num_segments=part_rows)
        border_grad = border_grad + jax.ops.segment_sum(grad_send[local_rows:], cut_source, num_segments=N_DOM * BORDER)
        return (border_grad, (node_out, node_grad, grad_edge[:local_rows].astype(jnp.bfloat16), grad_edge[local_rows:].astype(jnp.bfloat16)))
    start_grad = jnp.zeros((N_DOM * BORDER, feat_width), jnp.float32)
    border_grad, results = lax.scan(one_partition, start_grad, (node_tables, local_blocks, cut_blocks, local_sources, local_targets, cut_sources, cut_targets, cut_live, cot_blocks))
    node_outs, node_grads, local_grads, cut_grads = results
    node_grads = jnp.concatenate([node_grads[:, :BORDER] + border_grad.reshape(N_DOM, BORDER, feat_width), node_grads[:, BORDER:]], axis=1)
    node_out = node_outs.reshape(N_DOM * part_rows, feat_width)
    node_grad = node_grads.reshape(N_DOM * part_rows, feat_width)
    local_grad = local_grads.reshape(N_DOM * local_rows, feat_width)
    cut_grad = cut_grads.reshape(N_DOM * N_FEAT * cut_rows, feat_width)
    return (node_out, node_grad, local_grad, cut_grad)
```

```python
import jax
import jax.numpy as jnp
from jax import lax
from jax.experimental import pallas as pl
from jax.experimental.pallas import tpu as pltpu
from jax.sharding import Mesh
from jax.sharding import PartitionSpec as P

Z, X, C, F = 8, 4, 2, 8
DOM = ("z", "x", "core")
D = 512
BORDER = 16
SLOTS = 16
OWN = 80
LOC = 128
CUT = 1024
ALL = LOC + CUT
PART = 640
GROUP = 256
GROUPS = CUT // GROUP
PACK = BORDER + 2
EPS = 1e-05
F32 = jnp.float32
BF16 = jnp.bfloat16


def dot(left, right):
    return jnp.dot(left, right, preferred_element_type=F32)


def dot_t(left, right):
    return lax.dot_general(left, right, (((1,), (1,)), ((), ())), preferred_element_type=F32)


def onehot(match):
    return jnp.where(match, 1.0, 0.0).astype(BF16)


def iota(shape, axis):
    return lax.broadcasted_iota(jnp.int32, shape, axis)


def normalize(values):
    centered = values - jnp.mean(values, axis=-1, keepdims=True)
    inv_std = lax.rsqrt(jnp.mean(centered * centered, axis=-1, keepdims=True) + EPS)
    return centered * inv_std, inv_std


def norm_back(scaled, normed, inv_std):
    first_mean = jnp.mean(scaled, axis=-1, keepdims=True)
    second_mean = jnp.mean(scaled * normed, axis=-1, keepdims=True)
    return inv_std * (scaled - first_mean - normed * second_mean)


def silu_and_slope(values):
    sigmoid = 0.5 * jnp.tanh(0.5 * values) + 0.5
    act = values * sigmoid
    return act.astype(BF16), sigmoid + act * (1.0 - sigmoid)


def split(values):
    upper = values.astype(BF16)
    return upper, (values - upper.astype(F32)).astype(BF16)


def prepare_body(
    nodes, border, lsend_col, lsend_row, recv_col, recv_row, sel_col, sel_row,
    senders, expand, spread, pick_t, send_t,
):
    pick = onehot(lsend_col[...] == iota((LOC, PART), 1))
    senders[0:LOC, :] = dot(pick, nodes[...]).astype(BF16)
    send_t[...] = onehot(lsend_row[...] == iota((PART, LOC), 0))
    expand[...] = onehot(recv_col[...] == (iota((ALL, 256), 1) & 127))
    spread[...] = onehot(recv_row[...] == iota((OWN, ALL), 0))
    for k in range(GROUPS):
        rows = slice(k * GROUP, (k + 1) * GROUP)
        table = jnp.concatenate(
            [border[c, x, 2 * k + dz, 0:BORDER, :] for dz in range(2) for x in range(X) for c in range(C)],
            axis=0,
        )
        pick = onehot(sel_col[rows, :] == iota((GROUP, GROUP), 1))
        senders[LOC + k * GROUP : LOC + (k + 1) * GROUP, :] = dot(pick, table).astype(BF16)
        pick_t[k, :, :] = onehot(sel_row[:, rows] == iota((GROUP, GROUP), 0))


def layer_body(
    core, weights, senders, local_edges, cut_edges, expand, spread, pick_t, send_t, own, cot,
    eb1, eb2, eg, es, nb1, nb2, ng, ns,
    node_out, local_grad, cut_grad, own_grad, keep, send, local_send,
    w1, w2, n1, n2, slope, normed, inv, sems,
):
    copies = []
    for f in range(F):
        for i, (ref, start, size) in enumerate(((w1, 0, 192), (w2, 192, 64), (n1, 256, 128), (n2, 384, 64))):
            copy = pltpu.make_async_copy(
                weights.at[f, pl.ds(start, size), :], ref.at[pl.ds(f * size, size), :], sems.at[i, f]
            )
            copy.start()
            copies.append((i, copy))

    def arrive(which):
        for i, copy in copies:
            if i == which:
                copy.wait()

    chunks = [(0, LOC, local_edges, 0)]
    chunks += [(LOC + k * GROUP, GROUP, cut_edges, k * GROUP) for k in range(GROUPS)]
    zeros = jnp.zeros((128 - OWN, D), BF16)

    arrive(0)
    received = dot(own[...], w1[2 * D : 3 * D, :]) + eb1[...]
    upper, lower = split(received)
    table = jnp.concatenate([upper, zeros, lower, zeros], axis=0)
    arrive(1)
    aggregate = jnp.zeros((OWN, D), F32)
    for row, count, edges, base in chunks:
        at = slice(row, row + count)
        edge = edges[base : base + count, :]
        pre = dot(edge, w1[0:D, :]) + dot(senders[at, :], w1[D : 2 * D, :]) + dot(expand[at, :], table)
        act, slope[at, :] = silu_and_slope(pre)
        unit, inv_std = normalize(dot(act, w2[...]) + eb2[...])
        normed[at, :] = unit
        inv[at, :] = inv_std
        message = edge.astype(F32) + unit * eg[...] + es[...]
        aggregate += dot(spread[:, at], message.astype(BF16))

    arrive(2)
    arrive(3)
    pre = dot(own[...], n1[0:D, :]) + dot(aggregate.astype(BF16), n1[D : 2 * D, :]) + nb1[...]
    act, node_slope = silu_and_slope(pre)
    unit, inv_std = normalize(dot(act, n2[...]) + nb2[...])
    node_out[...] = (own[...].astype(F32) + unit * ng[...] + ns[...]).astype(BF16)
    cotangent = cot[...].astype(F32)
    back = norm_back(cotangent * ng[...], unit, inv_std).astype(BF16)
    back = (dot_t(back, n2[...]) * node_slope).astype(BF16)
    result = cotangent + dot_t(back, n1[0:D, :])
    upper, lower = split(dot_t(back, n1[D : 2 * D, :]))
    table = jnp.concatenate([upper, zeros, lower, zeros], axis=0)

    received = jnp.zeros((OWN, D), F32)
    mine = core[0] == 0
    for index, (row, count, _, base) in enumerate(chunks):
        at = slice(row, row + count)
        grad = dot(expand[at, :], table)
        back = norm_back(grad * eg[...], normed[at, :], inv[at, :]).astype(BF16)
        back = (dot_t(back, w2[...]) * slope[at, :]).astype(BF16)
        edge_grad = (grad + dot_t(back, w1[0:D, :])).astype(BF16)
        send_grad = dot_t(back, w1[D : 2 * D, :]).astype(BF16)
        received += dot(spread[:, at], back)
        if index == 0:
            local_grad[...] = edge_grad
            local_send[...] = dot(send_t[...], send_grad).astype(BF16)
        else:
            cut_grad[base : base + count, :] = edge_grad
            summed = dot(pick_t[index - 1], send_grad)
            for dz in range(2):
                for x in range(X):
                    start = (dz * X + x) * C * BORDER
                    first = summed[start : start + BORDER, :]
                    second = summed[start + BORDER : start + 2 * BORDER, :]
                    to = (x * Z + 2 * (index - 1) + dz) * BORDER
                    keep[to : to + BORDER, :] = jnp.where(mine, first, second)
                    send[to : to + BORDER, :] = jnp.where(mine, second, first).astype(BF16)
    upper, lower = split(received)
    both = dot_t(jnp.concatenate([upper, lower], axis=0), w1[2 * D : 3 * D, :])
    own_grad[...] = result + both[0:OWN, :] + both[OWN : 2 * OWN, :]


def shape(*dims, kind=BF16):
    return jax.ShapeDtypeStruct(dims, kind)


VMEM = pl.BlockSpec(memory_space=pltpu.VMEM)


def prepare(*args):
    return pl.pallas_call(
        prepare_body,
        in_specs=[VMEM] * 8,
        out_specs=[VMEM] * 5,
        out_shape=[
            shape(ALL, D), shape(ALL, 256), shape(OWN, ALL), shape(GROUPS, GROUP, GROUP), shape(PART, LOC),
        ],
        compiler_params=pltpu.CompilerParams(vmem_limit_bytes=24 * 1024 * 1024),
        cost_estimate=pl.CostEstimate(flops=800_000_000, bytes_accessed=6_000_000, transcendentals=0),
        name="prepare",
    )(*args)


def layer(*args):
    return pl.pallas_call(
        layer_body,
        in_specs=[pl.BlockSpec(memory_space=pltpu.SMEM), pl.BlockSpec(memory_space=pl.ANY)] + [VMEM] * 17,
        out_specs=[VMEM] * 7,
        out_shape=[
            shape(OWN, D), shape(LOC, D), shape(CUT, D), shape(OWN, D, kind=F32),
            shape(CUT // 2, D, kind=F32), shape(CUT // 2, D), shape(PART, D),
        ],
        scratch_shapes=[
            pltpu.VMEM((3 * D, D), BF16),
            pltpu.VMEM((D, D), BF16),
            pltpu.VMEM((2 * D, D), BF16),
            pltpu.VMEM((D, D), BF16),
            pltpu.VMEM((ALL, D), F32),
            pltpu.VMEM((ALL, D), F32),
            pltpu.VMEM((ALL, 1), F32),
            pltpu.SemaphoreType.DMA((4, F)),
        ],
        compiler_params=pltpu.CompilerParams(vmem_limit_bytes=40 * 1024 * 1024),
        cost_estimate=pl.CostEstimate(flops=4_000_000_000, bytes_accessed=12_000_000, transcendentals=600_000),
        name="layer",
    )(*args)


def exchange(values, axis):
    return lax.all_to_all(values, axis, split_axis=0, concat_axis=0, tiled=True)


def shards(
    node_in, local_edges, cut_edges, node_cot, edge_w1, edge_w2, node_w1, node_w2,
    edge_b1, edge_b2, edge_gain, edge_shift, node_b1, node_b2, node_gain, node_shift,
    local_send, local_recv, cut_send, cut_recv, cut_count,
):
    feat = lax.axis_index("feat")
    core = lax.axis_index("core")
    partition = (lax.axis_index("z") * X + lax.axis_index("x")) * C + core
    packed = jnp.concatenate([edge_w1, edge_w2, node_w1, node_w2], axis=0)
    weights = lax.all_gather(packed, "feat", axis=0, tiled=False)

    selectors = cut_send[0, 0].astype(BF16).reshape(2, D)
    payload = jnp.concatenate([node_in[:BORDER], selectors], axis=0)
    payload = exchange(jnp.broadcast_to(payload[None], (Z, PACK, D)), "z")
    payload = exchange(jnp.broadcast_to(payload[None], (X, Z, PACK, D)), "x")
    other = lax.ppermute(payload, "core", [(0, 1), (1, 0)])
    border = jnp.where(core == 0, jnp.stack([payload, other]), jnp.stack([other, payload]))
    selectors = lax.dynamic_slice(
        border,
        (0, 0, 0, BORDER + partition // 32, (partition % 32) * SLOTS),
        (C, X, Z, 1, SLOTS),
    )
    selectors = selectors.reshape(C, X, Z, SLOTS).transpose(2, 1, 0, 3).reshape(CUT).astype(jnp.int32)
    selectors = selectors + (jnp.arange(CUT, dtype=jnp.int32) % GROUP) // SLOTS * SLOTS

    live = jnp.arange(SLOTS, dtype=jnp.int32)[None, :] < cut_count[0, 0][:, None]
    receivers = jnp.concatenate([local_recv, jnp.where(live.reshape(-1), cut_recv[0, 0], -1)])
    senders, expand, spread, pick_t, send_t = prepare(
        node_in, border, local_send[:, None], local_send[None, :], receivers[:, None], receivers[None, :],
        selectors[:, None], selectors[None, :],
    )
    own = lax.dynamic_slice_in_dim(node_in, feat * OWN, OWN, 0)
    vectors = [
        v[None, :]
        for v in (edge_b1, edge_b2, edge_gain, edge_shift, node_b1, node_b2, node_gain, node_shift)
    ]
    node_out, local_grad, cut_grad, own_grad, keep, send, local_sums = layer(
        core.astype(jnp.int32).reshape(1), weights, senders, local_edges, cut_edges, expand, spread, pick_t,
        send_t, own, node_cot, *vectors,
    )
    scattered = lax.psum_scatter(local_sums, "feat", scatter_dimension=0, tiled=True)
    summed = keep + lax.ppermute(send, "core", [(0, 1), (1, 0)]).astype(F32)
    summed = exchange(summed.astype(BF16).reshape(X, Z * BORDER, D), "x")
    summed = jnp.sum(summed.astype(F32), axis=0)
    summed = exchange(summed.astype(BF16).reshape(Z, BORDER, D), "z")
    summed = jnp.sum(summed.astype(F32), axis=0).astype(BF16)
    summed = exchange(jnp.broadcast_to(summed[None], (F, BORDER, D)), "feat")
    summed = jnp.where(feat == 0, jnp.sum(summed.astype(F32), axis=0), 0.0)
    node_grad = own_grad + scattered.astype(F32) + jnp.pad(summed, ((0, OWN - BORDER), (0, 0)))
    return node_out, node_grad, local_grad, cut_grad


def solution(mesh):
    split_mesh = Mesh(mesh.devices.reshape(Z, X, C, F), (*DOM, "feat"))
    both = (*DOM, "feat")
    placed = (
        P(DOM, None),
        *[P(both, None)] * 3,
        *[P("feat", None)] * 4,
        *[P()] * 8,
        *[P(both)] * 2,
        *[P(DOM, "feat", None)] * 3,
    )
    return jax.shard_map(
        shards,
        mesh=split_mesh,
        in_specs=placed,
        out_specs=(P(both, None),) * 4,
        check_vma=False,
    )
```

```python
import jax
import jax.numpy as jnp
from jax import lax
from jax.experimental import pallas as pl
from jax.experimental.pallas import tpu as pltpu
from jax.sharding import Mesh
from jax.sharding import PartitionSpec as P

Z, X, C, F = 8, 4, 2, 8
DOM = ("z", "x", "core")
D = 512
BORDER = 16
SLOTS = 16
OWN = 80
LOC = 128
CUT = 1024
ALL = LOC + CUT
PART = 640
GROUP = 256
GROUPS = CUT // GROUP
PACK = BORDER + 8
EPS = 1e-05
LIMIT = 60 * 1024 * 1024
F32 = jnp.float32
BF16 = jnp.bfloat16


def dot(left, right):
    return jnp.dot(left, right, preferred_element_type=F32)


def dot_t(left, right):
    return lax.dot_general(left, right, (((1,), (1,)), ((), ())), preferred_element_type=F32)


def onehot(match):
    return jnp.where(match, 1.0, 0.0).astype(BF16)


def iota(shape, axis):
    return lax.broadcasted_iota(jnp.int32, shape, axis)


def normalize(values):
    centered = values - jnp.mean(values, axis=-1, keepdims=True)
    inv_std = lax.rsqrt(jnp.mean(centered * centered, axis=-1, keepdims=True) + EPS)
    return centered * inv_std, inv_std


def norm_back(scaled, normed, inv_std):
    first_mean = jnp.mean(scaled, axis=-1, keepdims=True)
    second_mean = jnp.mean(scaled * normed, axis=-1, keepdims=True)
    return inv_std * (scaled - first_mean - normed * second_mean)


def silu_and_slope(values):
    sigmoid = 0.5 * jnp.tanh(0.5 * values) + 0.5
    act = values * sigmoid
    return act.astype(BF16), sigmoid + act * (1.0 - sigmoid)


def split(values):
    upper = values.astype(BF16)
    return upper, (values - upper.astype(F32)).astype(BF16)


def index_body(
    feat, nodes, sent, moved, local_to, cut_to, counts, eb1, eb2, eg, es, nb1, nb2, ng, ns,
    senders, expand, spread, send_t, own, vectors,
):
    for i, vector in enumerate((eb1, eb2, eg, es, nb1, nb2, ng, ns)):
        vectors[i : i + 1, :] = vector[...]
    own[...] = nodes[pl.ds(pl.multiple_of(feat[0] * OWN, 16), OWN), :]
    pick = jnp.where(sent[...] == iota((PART, LOC), 0), 1.0, 0.0)
    senders[...] = dot(pick.T.astype(BF16), nodes[...]).astype(BF16)
    send_t[...] = onehot(moved[...] == iota((PART, LOC), 0))
    sources = CUT // SLOTS
    repeat = onehot(iota((sources, CUT), 1) // SLOTS == iota((sources, CUT), 0))
    count = dot(counts[...].astype(F32).astype(BF16), repeat)
    live = (iota((1, CUT), 1) & (SLOTS - 1)).astype(F32) < count
    cut = jnp.where(live, cut_to[...], -1)
    for start, count, to in ((0, LOC, local_to[...]), (LOC, CUT, cut)):
        match = jnp.where(to == iota((128, count), 0), 1.0, 0.0)
        spread[:, start : start + count] = match[0:OWN, :].astype(BF16)
        turned = match.T.astype(BF16)
        expand[start : start + count, 0:128] = turned
        expand[start : start + count, 128:256] = turned


def pick_body(where, near, far, senders, pick_t, selected):
    z, x, c = [where[i] for i in range(3)]
    partition = (z * X + x) * C + c
    tables = []
    for zz in range(Z):
        blocks = []
        for xx in range(X):
            step, turn = (x - xx + X) % X, (z + 1 - zz + Z) % Z
            pair = near[step, turn], far[step, turn]
            for cc in range(C):
                block = jnp.where(c == cc, pair[0], pair[1])
                blocks.append(block[0:BORDER, :])
                row = jnp.where(partition < 32, block[BORDER : BORDER + 1, :], block[BORDER + 1 : BORDER + 2, :])
                place = (zz * X + xx) * C + cc
                selected[place : place + 1, :] = row.astype(F32)
        tables.append(jnp.concatenate(blocks, axis=0))
    offset = (partition & 31) * SLOTS
    take = onehot(iota((D, GROUP), 0) == (iota((D, GROUP), 1) & (SLOTS - 1)) + offset)
    values = dot(selected[...].astype(BF16), take)
    lanes, rows = iota((SLOTS, GROUP), 1), iota((SLOTS, GROUP), 0)
    for k in range(GROUPS):
        group = values[k * SLOTS : (k + 1) * SLOTS, :]
        picked = jnp.sum(jnp.where(lanes // SLOTS == rows, group, 0.0), axis=0, keepdims=True)
        picked = picked.astype(jnp.int32) + iota((1, GROUP), 1) // SLOTS * SLOTS
        match = jnp.where(picked == iota((GROUP, GROUP), 0), 1.0, 0.0)
        pick_t[k, :, :] = match.astype(BF16)
        table = jnp.concatenate(tables[2 * k : 2 * k + 2], axis=0)
        senders[k * GROUP : (k + 1) * GROUP, :] = dot(match.T.astype(BF16), table).astype(BF16)


def layer_body(
    core, mine, other, local_edges, cut_edges, cot, local_senders, expand, spread, send_t, own, vectors,
    cut_senders, pick_t,
    node_out, local_grad, cut_grad, own_grad, keep, send, local_keep, local_send,
    w1, w2, n1, n2, edges, slope, normed, inv, sems, edge_sems,
):
    copies = []
    edge_copies = [
        pltpu.make_async_copy(local_edges, edges.at[pl.ds(0, LOC), :], edge_sems.at[0]),
        pltpu.make_async_copy(cut_edges, edges.at[pl.ds(LOC, CUT), :], edge_sems.at[1]),
    ]
    first = core[0]
    for i, (ref, start, size) in enumerate(((w1, 0, 96), (w2, 96, 32), (n1, 128, 64), (n2, 192, 32))):
        for f in range(F):
            for j, (half, place) in enumerate(((mine, first), (other, 1 - first))):
                to = pl.multiple_of((2 * f + place) * size, 32)
                copy = pltpu.make_async_copy(
                    half.at[f, pl.ds(start, size), :], ref.at[pl.ds(to, size), :], sems.at[i, f, j]
                )
                copy.start()
                copies.append((i, copy))
        if i == 0:
            for copy in edge_copies:
                copy.start()
    eb1, eb2, eg, es, nb1, nb2, ng, ns = [vectors.at[pl.ds(i, 1), :] for i in range(8)]

    def arrive(which):
        for i, copy in copies:
            if i == which:
                copy.wait()

    chunks = [(0, LOC)] + [(LOC + k * GROUP, GROUP) for k in range(GROUPS)]
    zeros = jnp.zeros((128 - OWN, D), BF16)

    arrive(0)
    received = dot(own[...], w1[2 * D : 3 * D, :]) + eb1[...]
    upper, lower = split(received)
    table = jnp.concatenate([upper, zeros, lower, zeros], axis=0)
    arrive(1)
    for copy in edge_copies:
        copy.wait()
    aggregate = jnp.zeros((OWN, D), F32)
    for row, count in chunks:
        at = slice(row, row + count)
        edge = edges[at, :]
        sender = local_senders[...] if row == 0 else cut_senders[row - LOC : row - LOC + count, :]
        pre = dot(edge, w1[0:D, :]) + dot(sender, w1[D : 2 * D, :]) + dot(expand[at, :], table)
        act, slope[at, :] = silu_and_slope(pre)
        unit, inv_std = normalize(dot(act, w2[...]) + eb2[...])
        normed[at, :] = unit
        inv[at, :] = inv_std
        message = edge.astype(F32) + unit * eg[...] + es[...]
        aggregate += dot(spread[:, at], message.astype(BF16))

    arrive(2)
    arrive(3)
    pre = dot(own[...], n1[0:D, :]) + dot(aggregate.astype(BF16), n1[D : 2 * D, :]) + nb1[...]
    act, node_slope = silu_and_slope(pre)
    unit, inv_std = normalize(dot(act, n2[...]) + nb2[...])
    node_out[...] = (own[...].astype(F32) + unit * ng[...] + ns[...]).astype(BF16)
    cotangent = cot[...].astype(F32)
    back = norm_back(cotangent * ng[...], unit, inv_std).astype(BF16)
    back = (dot_t(back, n2[...]) * node_slope).astype(BF16)
    result = cotangent + dot_t(back, n1[0:D, :])
    upper, lower = split(dot_t(back, n1[D : 2 * D, :]))
    table = jnp.concatenate([upper, zeros, lower, zeros], axis=0)

    received = jnp.zeros((OWN, D), F32)
    is_first = first == 0
    for index, (row, count) in enumerate(chunks):
        at = slice(row, row + count)
        grad = dot(expand[at, :], table)
        back = norm_back(grad * eg[...], normed[at, :], inv[at, :]).astype(BF16)
        back = (dot_t(back, w2[...]) * slope[at, :]).astype(BF16)
        edge_grad = (grad + dot_t(back, w1[0:D, :])).astype(BF16)
        send_grad = dot_t(back, w1[D : 2 * D, :]).astype(BF16)
        received += dot(spread[:, at], back)
        if index == 0:
            local_grad[...] = edge_grad
            by_owner = dot(send_t[...], send_grad)
            local_keep[...] = by_owner[0 : PART // 2, :]
            local_send[...] = by_owner[PART // 2 : PART, :].astype(BF16)
        else:
            cut_grad[row - LOC : row - LOC + count, :] = edge_grad
            summed = dot(pick_t[index - 1], send_grad)
            for dz in range(2):
                for x in range(X):
                    start = (dz * X + x) * C * BORDER
                    near = summed[start : start + BORDER, :]
                    far = summed[start + BORDER : start + 2 * BORDER, :]
                    to = ((2 * (index - 1) + dz) * X + x) * BORDER
                    keep[to : to + BORDER, :] = jnp.where(is_first, near, far)
                    send[to : to + BORDER, :] = jnp.where(is_first, far, near).astype(BF16)
    upper, lower = split(received)
    both = dot_t(jnp.concatenate([upper, lower], axis=0), w1[2 * D : 3 * D, :])
    own_grad[...] = result + both[0:OWN, :] + both[OWN : 2 * OWN, :]


def shape(*dims, kind=BF16):
    return jax.ShapeDtypeStruct(dims, kind)


VMEM = pl.BlockSpec(memory_space=pltpu.VMEM)
SMEM = pl.BlockSpec(memory_space=pltpu.SMEM)
HBM = pl.BlockSpec(memory_space=pltpu.HBM)
ANY = pl.BlockSpec(memory_space=pl.ANY)


def index(*args):
    return pl.pallas_call(
        index_body,
        in_specs=[SMEM] + [VMEM] * 14,
        out_specs=[VMEM] * 6,
        out_shape=[
            shape(LOC, D), shape(ALL, 256), shape(OWN, ALL), shape(PART, LOC), shape(OWN, D), shape(8, D, kind=F32),
        ],
        compiler_params=pltpu.CompilerParams(vmem_limit_bytes=LIMIT),
        cost_estimate=pl.CostEstimate(flops=200_000_000, bytes_accessed=3_000_000, transcendentals=0),
        name="index",
    )(*args)


def pick(*args):
    return pl.pallas_call(
        pick_body,
        in_specs=[SMEM, VMEM, VMEM],
        out_specs=[VMEM] * 2,
        out_shape=[shape(CUT, D), shape(GROUPS, GROUP, GROUP)],
        scratch_shapes=[pltpu.VMEM((Z * X * C, D), F32)],
        compiler_params=pltpu.CompilerParams(vmem_limit_bytes=LIMIT),
        cost_estimate=pl.CostEstimate(flops=300_000_000, bytes_accessed=4_000_000, transcendentals=0),
        name="pick",
    )(*args)


def layer(*args):
    return pl.pallas_call(
        layer_body,
        in_specs=[SMEM] + [ANY] * 4 + [VMEM] * 9,
        out_specs=[VMEM] * 8,
        out_shape=[
            shape(OWN, D), shape(LOC, D), shape(CUT, D), shape(OWN, D, kind=F32),
            shape(CUT // 2, D, kind=F32), shape(CUT // 2, D),
            shape(PART // 2, D, kind=F32), shape(PART // 2, D),
        ],
        scratch_shapes=[
            pltpu.VMEM((3 * D, D), BF16),
            pltpu.VMEM((D, D), BF16),
            pltpu.VMEM((2 * D, D), BF16),
            pltpu.VMEM((D, D), BF16),
            pltpu.VMEM((ALL, D), BF16),
            pltpu.VMEM((ALL, D), F32),
            pltpu.VMEM((ALL, D), F32),
            pltpu.VMEM((ALL, 1), F32),
            pltpu.SemaphoreType.DMA((4, F, 2)),
            pltpu.SemaphoreType.DMA((2,)),
        ],
        compiler_params=pltpu.CompilerParams(vmem_limit_bytes=LIMIT),
        cost_estimate=pl.CostEstimate(flops=4_000_000_000, bytes_accessed=12_000_000, transcendentals=600_000),
        name="layer",
    )(*args)


def after_body(values, other, out):
    del values, other, out


def after(values, other):
    return pl.pallas_call(
        after_body,
        in_specs=[HBM, ANY],
        out_specs=HBM,
        out_shape=jax.ShapeDtypeStruct(values.shape, values.dtype),
        input_output_aliases={0: 0},
        cost_estimate=pl.CostEstimate(flops=0, bytes_accessed=0, transcendentals=0),
        name="after",
    )(values, other)


def pack_body(core, first, second, third, fourth, out, half, sems):
    start = 0
    for ref in (first, second, third, fourth):
        size = ref.shape[0] // C
        half[start : start + size, :] = ref[pl.ds(pl.multiple_of(core[0] * size, 32), size), :]
        start += size
    copies = [pltpu.make_async_copy(half, out.at[f], sems.at[f]) for f in range(F)]
    for copy in copies:
        copy.start()
    for copy in copies:
        copy.wait()


def pack(core, *parts):
    rows = sum(part.shape[0] for part in parts) // C
    return pl.pallas_call(
        pack_body,
        in_specs=[SMEM] + [VMEM] * 4,
        out_specs=HBM,
        out_shape=shape(F, rows, D),
        scratch_shapes=[pltpu.VMEM((rows, D), BF16), pltpu.SemaphoreType.DMA((F,))],
        compiler_params=pltpu.CompilerParams(vmem_limit_bytes=LIMIT),
        cost_estimate=pl.CostEstimate(flops=0, bytes_accessed=2_000_000, transcendentals=0),
        name="pack",
    )(core, *parts)


def shift(values, axis, size, step):
    return lax.ppermute(values, axis, [(i, (i + step) % size) for i in range(size)])


def exchange(values, axis):
    return lax.all_to_all(values, axis, split_axis=0, concat_axis=0, tiled=True)


def shards(
    node_in, local_edges, cut_edges, node_cot, edge_w1, edge_w2, node_w1, node_w2,
    edge_b1, edge_b2, edge_gain, edge_shift, node_b1, node_b2, node_gain, node_shift,
    local_send, local_recv, cut_send, cut_recv, cut_count,
):
    feat = lax.axis_index("feat")
    core = lax.axis_index("core")
    weights = exchange(pack(core.astype(jnp.int32).reshape(1), edge_w1, edge_w2, node_w1, node_w2), "feat")
    selectors = cut_send[0, 0].astype(BF16).reshape(2, D)
    selectors = jnp.pad(selectors, ((0, PACK - BORDER - 2), (0, 0)))
    payload = jnp.concatenate([node_in[:BORDER], selectors], axis=0)
    payload = jnp.stack([shift(payload, "z", Z, Z - 1), payload, shift(payload, "z", Z, 1)])
    payload = jnp.concatenate([payload, shift(payload, "z", Z, 3), shift(payload[1:], "z", Z, Z - 3)], axis=0)
    near = jnp.stack([payload] + [shift(payload, "x", X, step) for step in range(1, X)])
    far = shift(near, "core", C, 1)
    owner = jnp.bitwise_xor(local_send // OWN, feat.astype(jnp.int32))
    owner = (owner & 1) * 4 + (owner & 2) + (owner >> 2)
    relative = owner * OWN + local_send % OWN
    vectors = (edge_b1, edge_b2, edge_gain, edge_shift, node_b1, node_b2, node_gain, node_shift)
    indices = index(
        feat.astype(jnp.int32).reshape(1), node_in, local_send[None, :], relative[None, :], local_recv[None, :],
        cut_recv[0], cut_count[0], *[v[None, :] for v in vectors],
    )
    place = jnp.stack([lax.axis_index(axis) for axis in DOM]).astype(jnp.int32)
    cut_senders, pick_t = pick(place, near, far)
    weights = after(weights, cut_senders)
    other_weights = shift(weights, "core", C, 1)
    node_out, local_grad, cut_grad, own_grad, keep, send, local_keep, local_sums = layer(
        core.astype(jnp.int32).reshape(1), weights, other_weights, local_edges, cut_edges, node_cot,
        *indices, cut_senders, pick_t,
    )
    summed = keep + lax.ppermute(send, "core", [(0, 1), (1, 0)]).astype(F32)
    for distance in (1, 2, 4):
        if distance > 1:
            half = local_keep.shape[0] // 2
            local_keep, local_sums = local_keep[:half], local_keep[half:].astype(BF16)
        arrived = lax.ppermute(local_sums, "feat", [(f, f ^ distance) for f in range(F)])
        local_keep = local_keep + arrived.astype(F32)
    summed = summed.astype(BF16)
    summed = exchange(summed.reshape(Z * X, BORDER, D), ("z", "x"))
    summed = jnp.sum(summed.astype(F32), axis=0).astype(BF16)
    summed = exchange(jnp.broadcast_to(summed[None], (F, BORDER, D)), "feat")
    summed = jnp.where(feat == 0, jnp.sum(summed.astype(F32), axis=0), 0.0)
    node_grad = own_grad + local_keep + jnp.pad(summed, ((0, OWN - BORDER), (0, 0)))
    return node_out, node_grad, local_grad, cut_grad


def solution(mesh):
    split_mesh = Mesh(mesh.devices.reshape(Z, X, C, F), (*DOM, "feat"))
    both = (*DOM, "feat")
    placed = (
        P(DOM, None),
        *[P(both, None)] * 3,
        *[P("feat", None)] * 4,
        *[P()] * 8,
        *[P(both)] * 2,
        *[P(DOM, "feat", None)] * 3,
    )
    return jax.shard_map(
        shards,
        mesh=split_mesh,
        in_specs=placed,
        out_specs=(P(both, None),) * 4,
        check_vma=False,
    )
```

```python
import jax
import jax.numpy as jnp
from jax import lax
from jax.experimental import pallas as pl
from jax.experimental.pallas import tpu as pltpu
from jax.sharding import Mesh
from jax.sharding import PartitionSpec as P

Z, X, C, F = 8, 4, 2, 8
DOM = ("z", "x", "core")
D = 512
BORDER = 16
SLOTS = 16
OWN = 80
LOC = 128
CUT = 1024
ALL = LOC + CUT
PART = 640
GROUP = 256
GROUPS = CUT // GROUP
CHUNK = 512
PACK = BORDER + 8
EPS = 1e-05
LIMIT = 65_500_000
F32 = jnp.float32
BF16 = jnp.bfloat16


def dot(left, right):
    return jnp.dot(left, right, preferred_element_type=F32)


def dot_t(left, right):
    return lax.dot_general(left, right, (((1,), (1,)), ((), ())), preferred_element_type=F32)


def onehot(match):
    return jnp.where(match, 1.0, 0.0).astype(BF16)


def iota(shape, axis):
    return lax.broadcasted_iota(jnp.int32, shape, axis)


def normalize(values):
    centered = values - jnp.mean(values, axis=-1, keepdims=True)
    inv_std = lax.rsqrt(jnp.mean(centered * centered, axis=-1, keepdims=True) + EPS)
    return centered * inv_std, inv_std


def norm_back(scaled, normed, inv_std):
    first_mean = jnp.mean(scaled, axis=-1, keepdims=True)
    second_mean = jnp.mean(scaled * normed, axis=-1, keepdims=True)
    return inv_std * (scaled - first_mean - normed * second_mean)


def silu_and_slope(values):
    sigmoid = 0.5 * jnp.tanh(0.5 * values) + 0.5
    act = values * sigmoid
    return act.astype(BF16), sigmoid + act * (1.0 - sigmoid)


def split(values):
    upper = values.astype(BF16)
    return upper, (values - upper.astype(F32)).astype(BF16)


def index_body(
    feat, nodes, sent, moved, local_to, cut_to, counts, eb1, eb2, eg, es, nb1, nb2, ng, ns,
    senders, expand, spread, send_t, own, vectors,
):
    for i, vector in enumerate((eb1, eb2, eg, es, nb1, nb2, ng, ns)):
        vectors[i : i + 1, :] = vector[...]
    own[...] = nodes[pl.ds(pl.multiple_of(feat[0] * OWN, 16), OWN), :]
    pick = jnp.where(sent[...] == iota((PART, LOC), 0), 1.0, 0.0)
    senders[...] = dot(pick.T.astype(BF16), nodes[...]).astype(BF16)
    send_t[...] = onehot(moved[...] == iota((PART, LOC), 0))
    sources = CUT // SLOTS
    repeat = onehot(iota((sources, CUT), 1) // SLOTS == iota((sources, CUT), 0))
    count = dot(counts[...].astype(F32).astype(BF16), repeat)
    live = (iota((1, CUT), 1) & (SLOTS - 1)).astype(F32) < count
    cut = jnp.where(live, cut_to[...], -1)
    for start, count, to in ((0, LOC, local_to[...]), (LOC, CUT, cut)):
        match = jnp.where(to == iota((128, count), 0), 1.0, 0.0)
        spread[:, start : start + count] = match[0:OWN, :].astype(BF16)
        turned = match.T.astype(BF16)
        expand[start : start + count, 0:128] = turned
        expand[start : start + count, 128:256] = turned


def pick_senders(where, near, far, senders, pick_t, selected):
    z, x, c = [where[i] for i in range(3)]
    partition = (z * X + x) * C + c
    tables = []
    for zz in range(Z):
        blocks = []
        for xx in range(X):
            step, turn = (x - xx + X) % X, (z + 1 - zz + Z) % Z
            pair = near[step, turn], far[step, turn]
            for cc in range(C):
                block = jnp.where(c == cc, pair[0], pair[1])
                blocks.append(block[0:BORDER, :])
                row = jnp.where(partition < 32, block[BORDER : BORDER + 1, :], block[BORDER + 1 : BORDER + 2, :])
                place = (zz * X + xx) * C + cc
                selected[place : place + 1, :] = row.astype(F32)
        tables.append(jnp.concatenate(blocks, axis=0))
    offset = (partition & 31) * SLOTS
    take = onehot(iota((D, GROUP), 0) == (iota((D, GROUP), 1) & (SLOTS - 1)) + offset)
    values = dot(selected[...].astype(BF16), take)
    lanes, rows = iota((SLOTS, GROUP), 1), iota((SLOTS, GROUP), 0)
    for k in range(GROUPS):
        group = values[k * SLOTS : (k + 1) * SLOTS, :]
        picked = jnp.sum(jnp.where(lanes // SLOTS == rows, group, 0.0), axis=0, keepdims=True)
        picked = picked.astype(jnp.int32) + iota((1, GROUP), 1) // SLOTS * SLOTS
        match = jnp.where(picked == iota((GROUP, GROUP), 0), 1.0, 0.0)
        pick_t[k, :, :] = match.astype(BF16)
        table = jnp.concatenate(tables[2 * k : 2 * k + 2], axis=0)
        senders[LOC + k * GROUP : LOC + (k + 1) * GROUP, :] = dot(match.T.astype(BF16), table).astype(BF16)


INPUTS = 13
OUTPUTS = 8
WEIGHTS = ((0, 96), (96, 32), (128, 64), (192, 32))


def layer_body(where, *refs):
    inputs, refs = refs[:INPUTS], refs[INPUTS:]
    outputs, scratch = refs[:OUTPUTS], refs[OUTPUTS:]
    mine, other, near_in, far_in, local_edges, cut_edges, local_senders, *small = inputs
    node_out, local_grad, cut_grad, own_grad, keep, send, local_keep, local_send = outputs
    near, far, edges, senders, expand, spread, send_t, own, cot, vectors, *scratch = scratch
    w1, w2, n1, n2, pick_t, selected, slope, normed, inv, *scratch = scratch
    node_out_v, own_grad_v, keep_v, send_v, local_keep_v, local_send_v, in_sems, w_sems, out_sems = scratch
    c = where[2]

    copies = [
        pltpu.make_async_copy(source, to, in_sems.at[i])
        for i, (source, to) in enumerate(
            (
                (near_in, near),
                (far_in, far),
                (local_edges, edges.at[pl.ds(0, LOC), :]),
                (cut_edges, edges.at[pl.ds(LOC, CUT), :]),
                (local_senders, senders.at[pl.ds(0, LOC), :]),
                *zip(small, (expand, spread, send_t, own, vectors, cot)),
            )
        )
    ]
    weight_copies = [
        [
            pltpu.make_async_copy(half.at[:, pl.ds(start, size), :], ref.at[:, place], w_sems.at[i, j])
            for j, (half, place) in enumerate(((mine, c), (other, 1 - c)))
        ]
        for i, (ref, (start, size)) in enumerate(zip((w1, w2, n1, n2), WEIGHTS))
    ]
    for copy in (*copies[:2], *weight_copies[0], *copies[2:], *weight_copies[1], *weight_copies[2], *weight_copies[3]):
        copy.start()
    leaving = []

    def leave(source, to):
        copy = pltpu.make_async_copy(source, to, out_sems.at[len(leaving)])
        copy.start()
        leaving.append(copy)

    def whole(ref):
        return ref[...].reshape(-1, D)

    for copy in copies[:2]:
        copy.wait()
    pick_senders(where, near, far, senders, pick_t, selected)
    eb1, eb2, eg, es, nb1, nb2, ng, ns = [vectors.at[pl.ds(i, 1), :] for i in range(8)]
    forward = ((0, LOC + CUT // 2), (LOC + CUT // 2, CUT // 2))
    chunks = ((0, LOC), (LOC, CUT))
    zeros = jnp.zeros((128 - OWN, D), BF16)

    for copy in (*copies[2:], *weight_copies[0]):
        copy.wait()
    first = whole(w1)
    first_edge, first_send, first_recv = first[0:D], first[D : 2 * D], first[2 * D : 3 * D]
    received = dot(own[...], first_recv) + eb1[...]
    upper, lower = split(received)
    table = jnp.concatenate([upper, zeros, lower, zeros], axis=0)
    for copy in weight_copies[1]:
        copy.wait()
    second = whole(w2)
    aggregate = jnp.zeros((OWN, D), F32)
    for row, count in forward:
        at = slice(row, row + count)
        edge = edges[at, :]
        pre = dot(edge, first_edge) + dot(senders[at, :], first_send) + dot(expand[at, :], table)
        act, slope[at, :] = silu_and_slope(pre)
        unit, inv_std = normalize(dot(act, second) + eb2[...])
        normed[at, :] = unit
        inv[at, :] = inv_std
        message = edge.astype(F32) + unit * eg[...] + es[...]
        aggregate += dot(spread[:, at], message.astype(BF16))

    for copy in (*weight_copies[2], *weight_copies[3]):
        copy.wait()
    node_first, node_second = whole(n1), whole(n2)
    pre = dot(own[...], node_first[0:D]) + dot(aggregate.astype(BF16), node_first[D : 2 * D]) + nb1[...]
    act, node_slope = silu_and_slope(pre)
    unit, inv_std = normalize(dot(act, node_second) + nb2[...])
    node_out_v[...] = (own[...].astype(F32) + unit * ng[...] + ns[...]).astype(BF16)
    leave(node_out_v, node_out)
    cotangent = cot[...].astype(F32)
    back = norm_back(cotangent * ng[...], unit, inv_std).astype(BF16)
    back = (dot_t(back, node_second) * node_slope).astype(BF16)
    upper, lower = split(dot_t(back, node_first[D : 2 * D]))
    table = jnp.concatenate([upper, zeros, lower, zeros], axis=0)
    result = cotangent + dot_t(back, node_first[0:D])

    received = jnp.zeros((OWN, D), F32)
    is_first = c == 0
    for index, (row, count) in enumerate(chunks):
        at = slice(row, row + count)
        grad = dot(expand[at, :], table)
        back = norm_back(grad * eg[...], normed[at, :], inv[at, :]).astype(BF16)
        back = (dot_t(back, second) * slope[at, :]).astype(BF16)
        edges[at, :] = (grad + dot_t(back, first_edge)).astype(BF16)
        send_grad = dot_t(back, first_send).astype(BF16)
        received += dot(spread[:, at], back)
        if index == 0:
            leave(edges.at[pl.ds(0, LOC), :], local_grad)
            by_owner = dot(send_t[...], send_grad)
            local_keep_v[...] = by_owner[0 : PART // 2, :]
            local_send_v[...] = by_owner[PART // 2 : PART, :].astype(BF16)
            leave(local_keep_v, local_keep)
            leave(local_send_v, local_send)
        else:
            leave(edges.at[pl.ds(row, count), :], cut_grad.at[pl.ds(row - LOC, count), :])
            base = (row - LOC) // C
            for k in range(count // GROUP):
                summed = dot(pick_t[(row - LOC) // GROUP + k], send_grad[k * GROUP : (k + 1) * GROUP])
                for place in range(2 * X):
                    near_sum = summed[place * C * BORDER : (place * C + 1) * BORDER, :]
                    far_sum = summed[(place * C + 1) * BORDER : (place + 1) * C * BORDER, :]
                    to = base + (k * 2 * X + place) * BORDER
                    keep_v[to : to + BORDER, :] = jnp.where(is_first, near_sum, far_sum).astype(BF16)
                    send_v[to : to + BORDER, :] = jnp.where(is_first, far_sum, near_sum).astype(BF16)
            part = pl.ds(base, count // C)
            leave(send_v.at[part, :], send.at[part, :])
            leave(keep_v.at[part, :], keep.at[part, :])
    upper, lower = split(received)
    both = dot_t(jnp.concatenate([upper, lower], axis=0), first_recv)
    own_grad_v[...] = result + both[0:OWN, :] + both[OWN : 2 * OWN, :]
    leave(own_grad_v, own_grad)
    for copy in leaving:
        copy.wait()


def shape(*dims, kind=BF16):
    return jax.ShapeDtypeStruct(dims, kind)


VMEM = pl.BlockSpec(memory_space=pltpu.VMEM)
SMEM = pl.BlockSpec(memory_space=pltpu.SMEM)
HBM = pl.BlockSpec(memory_space=pltpu.HBM)
ANY = pl.BlockSpec(memory_space=pl.ANY)


def index(*args):
    return pl.pallas_call(
        index_body,
        in_specs=[SMEM] + [VMEM] * 14,
        out_specs=[VMEM] * 6,
        out_shape=[
            shape(LOC, D), shape(ALL, 256), shape(OWN, ALL), shape(PART, LOC), shape(OWN, D), shape(8, D, kind=F32),
        ],
        compiler_params=pltpu.CompilerParams(vmem_limit_bytes=LIMIT),
        cost_estimate=pl.CostEstimate(flops=200_000_000, bytes_accessed=3_000_000, transcendentals=0),
        name="index",
    )(*args)


def layer(*args):
    return pl.pallas_call(
        layer_body,
        in_specs=[SMEM] + [ANY] * INPUTS,
        out_specs=[ANY] * OUTPUTS,
        out_shape=[
            shape(OWN, D), shape(LOC, D), shape(CUT, D), shape(OWN, D, kind=F32),
            shape(CUT // 2, D), shape(CUT // 2, D),
            shape(PART // 2, D, kind=F32), shape(PART // 2, D),
        ],
        scratch_shapes=[
            pltpu.VMEM((X, Z, PACK, D), BF16),
            pltpu.VMEM((X, Z, PACK, D), BF16),
            pltpu.VMEM((ALL, D), BF16),
            pltpu.VMEM((ALL, D), BF16),
            pltpu.VMEM((ALL, 256), BF16),
            pltpu.VMEM((OWN, ALL), BF16),
            pltpu.VMEM((PART, LOC), BF16),
            pltpu.VMEM((OWN, D), BF16),
            pltpu.VMEM((OWN, D), BF16),
            pltpu.VMEM((8, D), F32),
            *[pltpu.VMEM((F, C, size, D), BF16) for _, size in WEIGHTS],
            pltpu.VMEM((GROUPS, GROUP, GROUP), BF16),
            pltpu.VMEM((Z * X * C, D), F32),
            pltpu.VMEM((ALL, D), F32),
            pltpu.VMEM((ALL, D), F32),
            pltpu.VMEM((ALL, 1), F32),
            pltpu.VMEM((OWN, D), BF16),
            pltpu.VMEM((OWN, D), F32),
            pltpu.VMEM((CUT // 2, D), BF16),
            pltpu.VMEM((CUT // 2, D), BF16),
            pltpu.VMEM((PART // 2, D), F32),
            pltpu.VMEM((PART // 2, D), BF16),
            pltpu.SemaphoreType.DMA((11,)),
            pltpu.SemaphoreType.DMA((4, C)),
            pltpu.SemaphoreType.DMA((17,)),
        ],
        compiler_params=pltpu.CompilerParams(vmem_limit_bytes=LIMIT),
        cost_estimate=pl.CostEstimate(flops=4_000_000_000, bytes_accessed=12_000_000, transcendentals=600_000),
        name="layer",
    )(*args)


def after_body(values, other, out):
    del values, other, out


def after(values, other):
    return pl.pallas_call(
        after_body,
        in_specs=[HBM, ANY],
        out_specs=HBM,
        out_shape=jax.ShapeDtypeStruct(values.shape, values.dtype),
        input_output_aliases={0: 0},
        compiler_params=pltpu.CompilerParams(vmem_limit_bytes=LIMIT),
        cost_estimate=pl.CostEstimate(flops=0, bytes_accessed=0, transcendentals=0),
        name="after",
    )(values, other)


def pack_body(core, first, second, third, fourth, out, half, sems):
    start = 0
    for ref in (first, second, third, fourth):
        size = ref.shape[0] // C
        half[start : start + size, :] = ref[pl.ds(pl.multiple_of(core[0] * size, 32), size), :]
        start += size
    copies = [pltpu.make_async_copy(half, out.at[f], sems.at[f]) for f in range(F)]
    for copy in copies:
        copy.start()
    for copy in copies:
        copy.wait()


def pack(core, *parts):
    rows = sum(part.shape[0] for part in parts) // C
    return pl.pallas_call(
        pack_body,
        in_specs=[SMEM] + [VMEM] * 4,
        out_specs=HBM,
        out_shape=shape(F, rows, D),
        scratch_shapes=[pltpu.VMEM((rows, D), BF16), pltpu.SemaphoreType.DMA((F,))],
        compiler_params=pltpu.CompilerParams(vmem_limit_bytes=LIMIT),
        cost_estimate=pl.CostEstimate(flops=0, bytes_accessed=2_000_000, transcendentals=0),
        name="pack",
    )(core, *parts)


def shift(values, axis, size, step):
    return lax.ppermute(values, axis, [(i, (i + step) % size) for i in range(size)])


def exchange(values, axis):
    return lax.all_to_all(values, axis, split_axis=0, concat_axis=0, tiled=True)


def shards(
    node_in, local_edges, cut_edges, node_cot, edge_w1, edge_w2, node_w1, node_w2,
    edge_b1, edge_b2, edge_gain, edge_shift, node_b1, node_b2, node_gain, node_shift,
    local_send, local_recv, cut_send, cut_recv, cut_count,
):
    feat = lax.axis_index("feat")
    core = lax.axis_index("core")
    weights = exchange(pack(core.astype(jnp.int32).reshape(1), edge_w1, edge_w2, node_w1, node_w2), "feat")
    selectors = cut_send[0, 0].astype(BF16).reshape(2, D)
    selectors = jnp.pad(selectors, ((0, PACK - BORDER - 2), (0, 0)))
    payload = jnp.concatenate([node_in[:BORDER], selectors], axis=0)
    payload = jnp.stack([shift(payload, "z", Z, Z - 1), payload, shift(payload, "z", Z, 1)])
    payload = jnp.concatenate([payload, shift(payload, "z", Z, 3), shift(payload[1:], "z", Z, Z - 3)], axis=0)
    near = jnp.stack([payload] + [shift(payload, "x", X, step) for step in range(1, X)])
    far = shift(near, "core", C, 1)
    owner = jnp.bitwise_xor(local_send // OWN, feat.astype(jnp.int32))
    owner = (owner & 1) * 4 + (owner & 2) + (owner >> 2)
    relative = owner * OWN + local_send % OWN
    vectors = (edge_b1, edge_b2, edge_gain, edge_shift, node_b1, node_b2, node_gain, node_shift)
    indices = index(
        feat.astype(jnp.int32).reshape(1), node_in, local_send[None, :], relative[None, :], local_recv[None, :],
        cut_recv[0], cut_count[0], *[v[None, :] for v in vectors],
    )
    place = jnp.stack([lax.axis_index(axis) for axis in DOM]).astype(jnp.int32)
    weights = after(weights, far)
    other_weights = shift(weights, "core", C, 1)
    node_out, local_grad, cut_grad, own_grad, keep, send, local_keep, local_sums = layer(
        place, weights, other_weights, near, far, local_edges, cut_edges, *indices, node_cot
    )
    summed = keep.astype(F32) + lax.ppermute(send, "core", [(0, 1), (1, 0)]).astype(F32)
    for distance in (1, 2, 4):
        if distance > 1:
            half = local_keep.shape[0] // 2
            local_keep, local_sums = local_keep[:half], local_keep[half:].astype(BF16)
        arrived = lax.ppermute(local_sums, "feat", [(f, f ^ distance) for f in range(F)])
        local_keep = local_keep + arrived.astype(F32)
    summed = summed.astype(BF16)
    summed = exchange(summed.reshape(Z * X, BORDER, D), ("z", "x"))
    summed = jnp.sum(summed.astype(F32), axis=0).astype(BF16)
    summed = exchange(jnp.broadcast_to(summed[None], (F, BORDER, D)), "feat")
    summed = jnp.where(feat == 0, jnp.sum(summed.astype(F32), axis=0), 0.0)
    node_grad = own_grad + local_keep + jnp.pad(summed, ((0, OWN - BORDER), (0, 0)))
    return node_out, node_grad, local_grad, cut_grad


def solution(mesh):
    split_mesh = Mesh(mesh.devices.reshape(Z, X, C, F), (*DOM, "feat"))
    both = (*DOM, "feat")
    placed = (
        P(DOM, None),
        *[P(both, None)] * 3,
        *[P("feat", None)] * 4,
        *[P()] * 8,
        *[P(both)] * 2,
        *[P(DOM, "feat", None)] * 3,
    )
    return jax.shard_map(
        shards,
        mesh=split_mesh,
        in_specs=placed,
        out_specs=(P(both, None),) * 4,
        check_vma=False,
    )
```

```python
import jax
import jax.numpy as jnp
from jax import lax
from jax.experimental import pallas as pl
from jax.experimental.pallas import tpu as pltpu
from jax.sharding import Mesh
from jax.sharding import PartitionSpec as P

Z, X, C, F = 8, 4, 2, 8
DOM = ("z", "x", "core")
D = 512
BORDER = 16
SLOTS = 16
OWN = 80
LOC = 128
CUT = 1024
ALL = LOC + CUT
PART = 640
GROUP = 256
GROUPS = CUT // GROUP
CHUNK = 512
PACK = BORDER + 8
EPS = 1e-05
LIMIT = 65_500_000
F32 = jnp.float32
BF16 = jnp.bfloat16


def dot(left, right):
    return jnp.dot(left, right, preferred_element_type=F32)


def dot_t(left, right):
    return lax.dot_general(left, right, (((1,), (1,)), ((), ())), preferred_element_type=F32)


def onehot(match):
    return jnp.where(match, 1.0, 0.0).astype(BF16)


def iota(shape, axis):
    return lax.broadcasted_iota(jnp.int32, shape, axis)


def normalize(values):
    centered = values - jnp.mean(values, axis=-1, keepdims=True)
    inv_std = lax.rsqrt(jnp.mean(centered * centered, axis=-1, keepdims=True) + EPS)
    return centered * inv_std, inv_std


def norm_back(scaled, normed, inv_std):
    first_mean = jnp.mean(scaled, axis=-1, keepdims=True)
    second_mean = jnp.mean(scaled * normed, axis=-1, keepdims=True)
    return inv_std * (scaled - first_mean - normed * second_mean)


def silu_and_slope(values):
    sigmoid = 0.5 * jnp.tanh(0.5 * values) + 0.5
    act = values * sigmoid
    return act.astype(BF16), sigmoid + act * (1.0 - sigmoid)


def split(values):
    upper = values.astype(BF16)
    return upper, (values - upper.astype(F32)).astype(BF16)


def index_body(
    feat, nodes, sent, moved, local_to, cut_to, counts, eb1, eb2, eg, es, nb1, nb2, ng, ns,
    senders, expand, spread, send_t, own, vectors,
):
    for i, vector in enumerate((eb1, eb2, eg, es, nb1, nb2, ng, ns)):
        vectors[i : i + 1, :] = vector[...]
    own[...] = nodes[pl.ds(pl.multiple_of(feat[0] * OWN, 16), OWN), :]
    pick = jnp.where(sent[...] == iota((PART, LOC), 0), 1.0, 0.0)
    senders[...] = dot(pick.T.astype(BF16), nodes[...]).astype(BF16)
    send_t[...] = onehot(moved[...] == iota((PART, LOC), 0))
    sources = CUT // SLOTS
    repeat = onehot(iota((sources, CUT), 1) // SLOTS == iota((sources, CUT), 0))
    count = dot(counts[...].astype(F32).astype(BF16), repeat)
    live = (iota((1, CUT), 1) & (SLOTS - 1)).astype(F32) < count
    cut = jnp.where(live, cut_to[...], -1)
    for start, count, to in ((0, LOC, local_to[...]), (LOC, CUT, cut)):
        match = jnp.where(to == iota((128, count), 0), 1.0, 0.0)
        spread[:, start : start + count] = match[0:OWN, :].astype(BF16)
        turned = match.T.astype(BF16)
        expand[start : start + count, :] = turned


def pick_senders(where, near, far, senders, pick_t, selected):
    z, x, c = [where[i] for i in range(3)]
    partition = (z * X + x) * C + c
    tables = []
    for zz in range(Z):
        blocks = []
        for xx in range(X):
            step, turn = (x - xx + X) % X, (z + 1 - zz + Z) % Z
            pair = near[step, turn], far[step, turn]
            for cc in range(C):
                block = jnp.where(c == cc, pair[0], pair[1])
                blocks.append(block[0:BORDER, :])
                row = jnp.where(partition < 32, block[BORDER : BORDER + 1, :], block[BORDER + 1 : BORDER + 2, :])
                place = (zz * X + xx) * C + cc
                selected[place : place + 1, :] = row.astype(F32)
        tables.append(jnp.concatenate(blocks, axis=0))
    offset = (partition & 31) * SLOTS
    take = onehot(iota((D, GROUP), 0) == (iota((D, GROUP), 1) & (SLOTS - 1)) + offset)
    values = dot(selected[...].astype(BF16), take)
    lanes, rows = iota((SLOTS, GROUP), 1), iota((SLOTS, GROUP), 0)
    for k in range(GROUPS):
        group = values[k * SLOTS : (k + 1) * SLOTS, :]
        picked = jnp.sum(jnp.where(lanes // SLOTS == rows, group, 0.0), axis=0, keepdims=True)
        picked = picked.astype(jnp.int32) + iota((1, GROUP), 1) // SLOTS * SLOTS
        match = jnp.where(picked == iota((GROUP, GROUP), 0), 1.0, 0.0)
        pick_t[k, :, :] = match.astype(BF16)
        table = jnp.concatenate(tables[2 * k : 2 * k + 2], axis=0)
        senders[LOC + k * GROUP : LOC + (k + 1) * GROUP, :] = dot(match.T.astype(BF16), table).astype(BF16)


INPUTS = 13
OUTPUTS = 8
WEIGHTS = ((0, 96), (96, 32), (128, 64), (192, 32))


def layer_body(where, *refs):
    inputs, refs = refs[:INPUTS], refs[INPUTS:]
    outputs, scratch = refs[:OUTPUTS], refs[OUTPUTS:]
    mine, other, near_in, far_in, local_edges, cut_edges, local_senders, *small = inputs
    node_out, local_grad, cut_grad, own_grad, keep, send, local_keep, local_send = outputs
    near, far, edges, senders, expand, spread, send_t, own, cot, vectors, *scratch = scratch
    w1, w2, n1, n2, pick_t, selected, slope, normed, inv, *scratch = scratch
    node_out_v, own_grad_v, keep_v, send_v, local_keep_v, local_send_v, in_sems, w_sems, out_sems = scratch
    c = where[2]

    copies = [
        pltpu.make_async_copy(source, to, in_sems.at[i])
        for i, (source, to) in enumerate(
            (
                (near_in, near),
                (far_in, far),
                (local_edges, edges.at[pl.ds(0, LOC), :]),
                (cut_edges, edges.at[pl.ds(LOC, CUT), :]),
                (local_senders, senders.at[pl.ds(0, LOC), :]),
                *zip(small, (expand, spread, send_t, own, vectors, cot)),
            )
        )
    ]
    weight_copies = [
        [
            pltpu.make_async_copy(half.at[:, pl.ds(start, size), :], ref.at[:, place], w_sems.at[i, j])
            for j, (half, place) in enumerate(((mine, c), (other, 1 - c)))
        ]
        for i, (ref, (start, size)) in enumerate(zip((w1, w2, n1, n2), WEIGHTS))
    ]
    for copy in (*copies[:2], *weight_copies[0], *copies[2:7], *copies[8:10], *weight_copies[1]):
        copy.start()
    leaving = []

    def leave(source, to):
        copy = pltpu.make_async_copy(source, to, out_sems.at[len(leaving)])
        copy.start()
        leaving.append(copy)

    def whole(ref):
        return ref[...].reshape(-1, D)

    for copy in copies[:2]:
        copy.wait()
    pick_senders(where, near, far, senders, pick_t, selected)
    eb1, eb2, eg, es, nb1, nb2, ng, ns = [vectors.at[pl.ds(i, 1), :] for i in range(8)]
    forward = ((0, LOC + CUT // 2), (LOC + CUT // 2, CUT // 2))
    chunks = ((LOC, CUT // 2), (LOC + CUT // 2, CUT // 2), (0, LOC))
    zeros = jnp.zeros((128 - OWN, D), BF16)

    late = (*weight_copies[2], *weight_copies[3], copies[7], copies[10])
    for copy in (*copies[2:7], *copies[8:10], *weight_copies[0]):
        copy.wait()
    for copy in late:
        copy.start()
    first = whole(w1)
    first_edge, first_send, first_recv = first[0:D], first[D : 2 * D], first[2 * D : 3 * D]
    received = dot(own[...], first_recv) + eb1[...]
    upper, lower = split(received)
    table = jnp.concatenate([upper, zeros, lower, zeros], axis=0)
    for copy in weight_copies[1]:
        copy.wait()
    second = whole(w2)
    aggregate = jnp.zeros((OWN, D), F32)
    for row, count in forward:
        at = slice(row, row + count)
        edge = edges[at, :]
        pre = dot(edge, first_edge) + dot(senders[at, :], first_send) + dot(jnp.concatenate([expand[at, :]] * 2, axis=1), table)
        act, slope[at, :] = silu_and_slope(pre)
        unit, inv_std = normalize(dot(act, second) + eb2[...])
        normed[at, :] = unit
        inv[at, :] = inv_std
        message = edge.astype(F32) + unit * eg[...] + es[...]
        aggregate += dot(spread[:, at], message.astype(BF16))

    for copy in late:
        copy.wait()
    node_first, node_second = whole(n1), whole(n2)
    pre = dot(own[...], node_first[0:D]) + dot(aggregate.astype(BF16), node_first[D : 2 * D]) + nb1[...]
    act, node_slope = silu_and_slope(pre)
    unit, inv_std = normalize(dot(act, node_second) + nb2[...])
    node_out_v[...] = (own[...].astype(F32) + unit * ng[...] + ns[...]).astype(BF16)
    leave(node_out_v, node_out)
    cotangent = cot[...].astype(F32)
    back = norm_back(cotangent * ng[...], unit, inv_std).astype(BF16)
    back = (dot_t(back, node_second) * node_slope).astype(BF16)
    upper, lower = split(dot_t(back, node_first[D : 2 * D]))
    table = jnp.concatenate([upper, zeros, lower, zeros], axis=0)
    result = cotangent + dot_t(back, node_first[0:D])

    received = jnp.zeros((OWN, D), F32)
    is_first = c == 0
    for row, count in chunks:
        at = slice(row, row + count)
        grad = dot(jnp.concatenate([expand[at, :]] * 2, axis=1), table)
        back = norm_back(grad * eg[...], normed[at, :], inv[at, :]).astype(BF16)
        back = (dot_t(back, second) * slope[at, :]).astype(BF16)
        edges[at, :] = (grad + dot_t(back, first_edge)).astype(BF16)
        send_grad = dot_t(back, first_send).astype(BF16)
        received += dot(spread[:, at], back)
        if row == 0:
            leave(edges.at[pl.ds(0, LOC), :], local_grad)
            by_owner = dot(send_t[...], send_grad)
            local_keep_v[...] = by_owner[0 : PART // 2, :]
            local_send_v[...] = by_owner[PART // 2 : PART, :].astype(BF16)
            leave(local_keep_v, local_keep)
            leave(local_send_v, local_send)
        else:
            leave(edges.at[pl.ds(row, count), :], cut_grad.at[pl.ds(row - LOC, count), :])
            base = (row - LOC) // C
            for k in range(count // GROUP):
                summed = dot(pick_t[(row - LOC) // GROUP + k], send_grad[k * GROUP : (k + 1) * GROUP])
                for place in range(2 * X):
                    near_sum = summed[place * C * BORDER : (place * C + 1) * BORDER, :]
                    far_sum = summed[(place * C + 1) * BORDER : (place + 1) * C * BORDER, :]
                    to = base + (k * 2 * X + place) * BORDER
                    keep_v[to : to + BORDER, :] = jnp.where(is_first, near_sum, far_sum).astype(BF16)
                    send_v[to : to + BORDER, :] = jnp.where(is_first, far_sum, near_sum).astype(BF16)
            part = pl.ds(base, count // C)
            leave(send_v.at[part, :], send.at[part, :])
            leave(keep_v.at[part, :], keep.at[part, :])
    upper, lower = split(received)
    both = dot_t(jnp.concatenate([upper, lower], axis=0), first_recv)
    own_grad_v[...] = result + both[0:OWN, :] + both[OWN : 2 * OWN, :]
    leave(own_grad_v, own_grad)
    for copy in leaving:
        copy.wait()


def shape(*dims, kind=BF16):
    return jax.ShapeDtypeStruct(dims, kind)


VMEM = pl.BlockSpec(memory_space=pltpu.VMEM)
SMEM = pl.BlockSpec(memory_space=pltpu.SMEM)
HBM = pl.BlockSpec(memory_space=pltpu.HBM)
ANY = pl.BlockSpec(memory_space=pl.ANY)


def index(*args):
    return pl.pallas_call(
        index_body,
        in_specs=[SMEM] + [VMEM] * 14,
        out_specs=[VMEM] * 6,
        out_shape=[
            shape(LOC, D), shape(ALL, 128), shape(OWN, ALL), shape(PART, LOC), shape(OWN, D), shape(8, D, kind=F32),
        ],
        compiler_params=pltpu.CompilerParams(vmem_limit_bytes=LIMIT),
        cost_estimate=pl.CostEstimate(flops=200_000_000, bytes_accessed=3_000_000, transcendentals=0),
        name="index",
    )(*args)


def layer(*args):
    return pl.pallas_call(
        layer_body,
        in_specs=[SMEM] + [ANY] * INPUTS,
        out_specs=[ANY] * OUTPUTS,
        out_shape=[
            shape(OWN, D), shape(LOC, D), shape(CUT, D), shape(OWN, D, kind=F32),
            shape(CUT // 2, D), shape(CUT // 2, D),
            shape(PART // 2, D, kind=F32), shape(PART // 2, D),
        ],
        scratch_shapes=[
            pltpu.VMEM((X, Z, PACK, D), BF16),
            pltpu.VMEM((X, Z, PACK, D), BF16),
            pltpu.VMEM((ALL, D), BF16),
            pltpu.VMEM((ALL, D), BF16),
            pltpu.VMEM((ALL, 128), BF16),
            pltpu.VMEM((OWN, ALL), BF16),
            pltpu.VMEM((PART, LOC), BF16),
            pltpu.VMEM((OWN, D), BF16),
            pltpu.VMEM((OWN, D), BF16),
            pltpu.VMEM((8, D), F32),
            *[pltpu.VMEM((F, C, size, D), BF16) for _, size in WEIGHTS],
            pltpu.VMEM((GROUPS, GROUP, GROUP), BF16),
            pltpu.VMEM((Z * X * C, D), F32),
            pltpu.VMEM((ALL, D), F32),
            pltpu.VMEM((ALL, D), F32),
            pltpu.VMEM((ALL, 1), F32),
            pltpu.VMEM((OWN, D), BF16),
            pltpu.VMEM((OWN, D), F32),
            pltpu.VMEM((CUT // 2, D), BF16),
            pltpu.VMEM((CUT // 2, D), BF16),
            pltpu.VMEM((PART // 2, D), F32),
            pltpu.VMEM((PART // 2, D), BF16),
            pltpu.SemaphoreType.DMA((11,)),
            pltpu.SemaphoreType.DMA((4, C)),
            pltpu.SemaphoreType.DMA((17,)),
        ],
        compiler_params=pltpu.CompilerParams(vmem_limit_bytes=LIMIT),
        cost_estimate=pl.CostEstimate(flops=4_000_000_000, bytes_accessed=12_000_000, transcendentals=600_000),
        name="layer",
    )(*args)


def after_body(values, other, out):
    del values, other, out


def after(values, other):
    return pl.pallas_call(
        after_body,
        in_specs=[HBM, ANY],
        out_specs=HBM,
        out_shape=jax.ShapeDtypeStruct(values.shape, values.dtype),
        input_output_aliases={0: 0},
        compiler_params=pltpu.CompilerParams(vmem_limit_bytes=LIMIT),
        cost_estimate=pl.CostEstimate(flops=0, bytes_accessed=0, transcendentals=0),
        name="after",
    )(values, other)


def pack_body(core, first, second, third, fourth, out, half, sems):
    start = 0
    for ref in (first, second, third, fourth):
        size = ref.shape[0] // C
        half[start : start + size, :] = ref[pl.ds(pl.multiple_of(core[0] * size, 32), size), :]
        start += size
    copies = [pltpu.make_async_copy(half, out.at[f], sems.at[f]) for f in range(F)]
    for copy in copies:
        copy.start()
    for copy in copies:
        copy.wait()


def pack(core, *parts):
    rows = sum(part.shape[0] for part in parts) // C
    return pl.pallas_call(
        pack_body,
        in_specs=[SMEM] + [VMEM] * 4,
        out_specs=HBM,
        out_shape=shape(F, rows, D),
        scratch_shapes=[pltpu.VMEM((rows, D), BF16), pltpu.SemaphoreType.DMA((F,))],
        compiler_params=pltpu.CompilerParams(vmem_limit_bytes=LIMIT),
        cost_estimate=pl.CostEstimate(flops=0, bytes_accessed=2_000_000, transcendentals=0),
        name="pack",
    )(core, *parts)


def shift(values, axis, size, step):
    return lax.ppermute(values, axis, [(i, (i + step) % size) for i in range(size)])


def exchange(values, axis):
    return lax.all_to_all(values, axis, split_axis=0, concat_axis=0, tiled=True)


def shards(
    node_in, local_edges, cut_edges, node_cot, edge_w1, edge_w2, node_w1, node_w2,
    edge_b1, edge_b2, edge_gain, edge_shift, node_b1, node_b2, node_gain, node_shift,
    local_send, local_recv, cut_send, cut_recv, cut_count,
):
    feat = lax.axis_index("feat")
    core = lax.axis_index("core")
    weights = exchange(pack(core.astype(jnp.int32).reshape(1), edge_w1, edge_w2, node_w1, node_w2), "feat")
    selectors = cut_send[0, 0].astype(BF16).reshape(2, D)
    selectors = jnp.pad(selectors, ((0, PACK - BORDER - 2), (0, 0)))
    payload = jnp.concatenate([node_in[:BORDER], selectors], axis=0)
    payload = jnp.stack([shift(payload, "z", Z, Z - 1), payload, shift(payload, "z", Z, 1)])
    payload = jnp.concatenate([payload, shift(payload, "z", Z, 3), shift(payload[1:], "z", Z, Z - 3)], axis=0)
    near = jnp.stack([payload] + [shift(payload, "x", X, step) for step in range(1, X)])
    far = shift(near, "core", C, 1)
    owner = jnp.bitwise_xor(local_send // OWN, feat.astype(jnp.int32))
    owner = (owner & 1) * 4 + (owner & 2) + (owner >> 2)
    relative = owner * OWN + local_send % OWN
    vectors = (edge_b1, edge_b2, edge_gain, edge_shift, node_b1, node_b2, node_gain, node_shift)
    indices = index(
        feat.astype(jnp.int32).reshape(1), node_in, local_send[None, :], relative[None, :], local_recv[None, :],
        cut_recv[0], cut_count[0], *[v[None, :] for v in vectors],
    )
    place = jnp.stack([lax.axis_index(axis) for axis in DOM]).astype(jnp.int32)
    weights = after(weights, far)
    other_weights = shift(weights, "core", C, 1)
    node_out, local_grad, cut_grad, own_grad, keep, send, local_keep, local_sums = layer(
        place, weights, other_weights, near, far, local_edges, cut_edges, *indices, node_cot
    )
    summed = keep.astype(F32) + lax.ppermute(send, "core", [(0, 1), (1, 0)]).astype(F32)
    for distance in (1, 2, 4):
        if distance > 1:
            half = local_keep.shape[0] // 2
            local_keep, local_sums = local_keep[:half], local_keep[half:].astype(BF16)
        arrived = lax.ppermute(local_sums, "feat", [(f, f ^ distance) for f in range(F)])
        local_keep = local_keep + arrived.astype(F32)
    summed = summed.astype(BF16)
    summed = exchange(summed.reshape(Z * X, BORDER, D), ("z", "x"))
    summed = jnp.sum(summed.astype(F32), axis=0).astype(BF16)
    summed = exchange(jnp.broadcast_to(summed[None], (F, BORDER, D)), "feat")
    summed = jnp.where(feat == 0, jnp.sum(summed.astype(F32), axis=0), 0.0)
    node_grad = own_grad + local_keep + jnp.pad(summed, ((0, OWN - BORDER), (0, 0)))
    return node_out, node_grad, local_grad, cut_grad


def solution(mesh):
    split_mesh = Mesh(mesh.devices.reshape(Z, X, C, F), (*DOM, "feat"))
    both = (*DOM, "feat")
    placed = (
        P(DOM, None),
        *[P(both, None)] * 3,
        *[P("feat", None)] * 4,
        *[P()] * 8,
        *[P(both)] * 2,
        *[P(DOM, "feat", None)] * 3,
    )
    return jax.shard_map(
        shards,
        mesh=split_mesh,
        in_specs=placed,
        out_specs=(P(both, None),) * 4,
        check_vma=False,
    )
```

```python
import jax
import jax.numpy as jnp
from jax import lax
from jax.experimental import pallas as pl
from jax.experimental.pallas import tpu as pltpu
from jax.sharding import Mesh
from jax.sharding import PartitionSpec as P

Z, X, C, F = 8, 4, 2, 8
DOM = ("z", "x", "core")
D = 512
BORDER = 16
SLOTS = 16
OWN = 80
LOC = 128
CUT = 1024
ALL = LOC + CUT
PART = 640
GROUP = 256
GROUPS = CUT // GROUP
CHUNK = 512
PACK = BORDER + 8
EPS = 1e-05
LIMIT = 65_500_000
F32 = jnp.float32
BF16 = jnp.bfloat16


def dot(left, right):
    return jnp.dot(left, right, preferred_element_type=F32)


def dot_t(left, right):
    return lax.dot_general(left, right, (((1,), (1,)), ((), ())), preferred_element_type=F32)


def onehot(match):
    return jnp.where(match, 1.0, 0.0).astype(BF16)


def iota(shape, axis):
    return lax.broadcasted_iota(jnp.int32, shape, axis)


def normalize(values):
    centered = values - jnp.mean(values, axis=-1, keepdims=True)
    inv_std = lax.rsqrt(jnp.mean(centered * centered, axis=-1, keepdims=True) + EPS)
    return centered * inv_std, inv_std


def norm_back(scaled, normed, inv_std):
    first_mean = jnp.mean(scaled, axis=-1, keepdims=True)
    second_mean = jnp.mean(scaled * normed, axis=-1, keepdims=True)
    return inv_std * (scaled - first_mean - normed * second_mean)


def silu_and_slope(values):
    sigmoid = 0.5 * jnp.tanh(0.5 * values) + 0.5
    act = values * sigmoid
    return act.astype(BF16), sigmoid + act * (1.0 - sigmoid)


def split(values):
    upper = values.astype(BF16)
    return upper, (values - upper.astype(F32)).astype(BF16)


def index_body(
    feat, nodes, sent, moved, local_to, cut_to, counts, eb1, eb2, eg, es, nb1, nb2, ng, ns,
    senders, expand, spread, send_t, own, vectors,
):
    for i, vector in enumerate((eb1, eb2, eg, es, nb1, nb2, ng, ns)):
        vectors[i : i + 1, :] = vector[...]
    own[...] = nodes[pl.ds(pl.multiple_of(feat[0] * OWN, 16), OWN), :]
    pick = jnp.where(sent[...] == iota((PART, LOC), 0), 1.0, 0.0)
    senders[...] = dot(pick.T.astype(BF16), nodes[...]).astype(BF16)
    send_t[...] = onehot(moved[...] == iota((PART, LOC), 0))
    sources = CUT // SLOTS
    repeat = onehot(iota((sources, CUT), 1) // SLOTS == iota((sources, CUT), 0))
    count = dot(counts[...].astype(F32).astype(BF16), repeat)
    live = (iota((1, CUT), 1) & (SLOTS - 1)).astype(F32) < count
    cut = jnp.where(live, cut_to[...], -1)
    for start, count, to in ((0, LOC, local_to[...]), (LOC, CUT, cut)):
        match = jnp.where(to == iota((128, count), 0), 1.0, 0.0)
        spread[:, start : start + count] = match[0:OWN, :].astype(BF16)
        turned = match.T.astype(BF16)
        expand[start : start + count, :] = turned


def pick_senders(where, near, far, senders, pick_t, selected):
    z, x, c = [where[i] for i in range(3)]
    partition = (z * X + x) * C + c
    tables = []
    for zz in range(Z):
        blocks = []
        for xx in range(X):
            step, turn = (x - xx + X) % X, (z + 1 - zz + Z) % Z
            pair = near[step, turn], far[step, turn]
            for cc in range(C):
                block = jnp.where(c == cc, pair[0], pair[1])
                blocks.append(block[0:BORDER, :])
                row = jnp.where(partition < 32, block[BORDER : BORDER + 1, :], block[BORDER + 1 : BORDER + 2, :])
                place = (zz * X + xx) * C + cc
                selected[place : place + 1, :] = row.astype(F32)
        tables.append(jnp.concatenate(blocks, axis=0))
    offset = (partition & 31) * SLOTS
    take = onehot(iota((D, GROUP), 0) == (iota((D, GROUP), 1) & (SLOTS - 1)) + offset)
    values = dot(selected[...].astype(BF16), take)
    lanes, rows = iota((SLOTS, GROUP), 1), iota((SLOTS, GROUP), 0)
    for k in range(GROUPS):
        group = values[k * SLOTS : (k + 1) * SLOTS, :]
        picked = jnp.sum(jnp.where(lanes // SLOTS == rows, group, 0.0), axis=0, keepdims=True)
        picked = picked.astype(jnp.int32) + iota((1, GROUP), 1) // SLOTS * SLOTS
        match = jnp.where(picked == iota((GROUP, GROUP), 0), 1.0, 0.0)
        pick_t[k, :, :] = match.astype(BF16)
        table = jnp.concatenate(tables[2 * k : 2 * k + 2], axis=0)
        senders[LOC + k * GROUP : LOC + (k + 1) * GROUP, :] = dot(match.T.astype(BF16), table).astype(BF16)


INPUTS = 13
OUTPUTS = 8
WEIGHTS = ((0, 96), (96, 32), (128, 64), (192, 32))


def layer_body(where, *refs):
    inputs, refs = refs[:INPUTS], refs[INPUTS:]
    outputs, scratch = refs[:OUTPUTS], refs[OUTPUTS:]
    mine, other, near_in, far_in, local_edges, cut_edges, local_senders, *small = inputs
    node_out, local_grad, cut_grad, own_grad, keep, send, local_keep, local_send = outputs
    near, far, edges, senders, expand, spread, send_t, own, cot, vectors, *scratch = scratch
    w1, w2, n1, n2, pick_t, selected, slope, normed, inv, *scratch = scratch
    node_out_v, own_grad_v, keep_v, send_v, local_keep_v, local_send_v, in_sems, w_sems, out_sems = scratch
    c = where[2]

    copies = [
        pltpu.make_async_copy(source, to, in_sems.at[i])
        for i, (source, to) in enumerate(
            (
                (near_in, near),
                (far_in, far),
                (local_edges, edges.at[pl.ds(0, LOC), :]),
                (cut_edges, edges.at[pl.ds(LOC, CUT), :]),
                (local_senders, senders.at[pl.ds(0, LOC), :]),
                *zip(small, (expand, spread, send_t, own, vectors, cot)),
            )
        )
    ]
    weight_copies = [
        [
            pltpu.make_async_copy(half.at[:, pl.ds(start, size), :], ref.at[:, place], w_sems.at[i, j])
            for j, (half, place) in enumerate(((mine, c), (other, 1 - c)))
        ]
        for i, (ref, (start, size)) in enumerate(zip((w1, w2, n1, n2), WEIGHTS))
    ]
    for copy in (*copies[:2], *weight_copies[0], *copies[2:7], *copies[8:10], *weight_copies[1]):
        copy.start()
    leaving = []

    def leave(source, to):
        copy = pltpu.make_async_copy(source, to, out_sems.at[len(leaving)])
        copy.start()
        leaving.append(copy)

    def whole(ref):
        return ref[...].reshape(-1, D)

    for copy in copies[:2]:
        copy.wait()
    pick_senders(where, near, far, senders, pick_t, selected)
    eb1, eb2, eg, es, nb1, nb2, ng, ns = [vectors.at[pl.ds(i, 1), :] for i in range(8)]
    forward = ((0, LOC + CUT // 2), (LOC + CUT // 2, CUT // 2))
    chunks = ((LOC, CUT // 2), (LOC + CUT // 2, CUT // 2), (0, LOC))
    zeros = jnp.zeros((128 - OWN, D), BF16)

    late = (*weight_copies[2], *weight_copies[3], copies[7], copies[10])
    for copy in (*copies[2:7], *copies[8:10], *weight_copies[0]):
        copy.wait()
    for copy in late:
        copy.start()
    first = whole(w1)
    first_edge, first_send, first_recv = first[0:D], first[D : 2 * D], first[2 * D : 3 * D]
    received = dot(own[...], first_recv) + eb1[...]
    upper, lower = split(received)
    table = jnp.concatenate([upper, zeros, lower, zeros], axis=0)
    for copy in weight_copies[1]:
        copy.wait()
    second = whole(w2)
    aggregate = jnp.zeros((OWN, D), F32)
    for row, count in forward:
        at = slice(row, row + count)
        edge = edges[at, :]
        pre = dot(edge, first_edge) + dot(senders[at, :], first_send) + dot(jnp.concatenate([expand[at, :]] * 2, axis=1), table)
        act, slope[at, :] = silu_and_slope(pre)
        unit, inv_std = normalize(dot(act, second) + eb2[...])
        normed[at, :] = unit
        inv[at, :] = inv_std
        message = edge.astype(F32) + unit * eg[...] + es[...]
        aggregate += dot(spread[:, at], message.astype(BF16))

    for copy in late:
        copy.wait()
    node_first, node_second = whole(n1), whole(n2)
    pre = dot(own[...], node_first[0:D]) + dot(aggregate.astype(BF16), node_first[D : 2 * D]) + nb1[...]
    act, node_slope = silu_and_slope(pre)
    unit, inv_std = normalize(dot(act, node_second) + nb2[...])
    node_out_v[...] = (own[...].astype(F32) + unit * ng[...] + ns[...]).astype(BF16)
    leave(node_out_v, node_out)
    cotangent = cot[...].astype(F32)
    back = norm_back(cotangent * ng[...], unit, inv_std).astype(BF16)
    back = (dot_t(back, node_second) * node_slope).astype(BF16)
    upper, lower = split(dot_t(back, node_first[D : 2 * D]))
    table = jnp.concatenate([upper, zeros, lower, zeros], axis=0)
    result = cotangent + dot_t(back, node_first[0:D])

    received = jnp.zeros((OWN, D), F32)
    is_first = c == 0
    for row, count in chunks:
        at = slice(row, row + count)
        grad = dot(jnp.concatenate([expand[at, :]] * 2, axis=1), table)
        back = norm_back(grad * eg[...], normed[at, :], inv[at, :]).astype(BF16)
        back = (dot_t(back, second) * slope[at, :]).astype(BF16)
        edges[at, :] = (grad + dot_t(back, first_edge)).astype(BF16)
        send_grad = dot_t(back, first_send).astype(BF16)
        received += dot(spread[:, at], back)
        if row == 0:
            leave(edges.at[pl.ds(0, LOC), :], local_grad)
            by_owner = dot(send_t[...], send_grad)
            local_keep_v[...] = by_owner[0 : PART // 2, :]
            local_send_v[...] = by_owner[PART // 2 : PART, :].astype(BF16)
            leave(local_keep_v, local_keep)
            leave(local_send_v, local_send)
        else:
            leave(edges.at[pl.ds(row, count), :], cut_grad.at[pl.ds(row - LOC, count), :])
            base = (row - LOC) // C
            for k in range(count // GROUP):
                summed = dot(pick_t[(row - LOC) // GROUP + k], send_grad[k * GROUP : (k + 1) * GROUP])
                for place in range(2 * X):
                    near_sum = summed[place * C * BORDER : (place * C + 1) * BORDER, :]
                    far_sum = summed[(place * C + 1) * BORDER : (place + 1) * C * BORDER, :]
                    to = base + (k * 2 * X + place) * BORDER
                    keep_v[to : to + BORDER, :] = jnp.where(is_first, near_sum, far_sum).astype(BF16)
                    send_v[to : to + BORDER, :] = jnp.where(is_first, far_sum, near_sum).astype(BF16)
            part = pl.ds(base, count // C)
            leave(send_v.at[part, :], send.at[part, :])
            leave(keep_v.at[part, :], keep.at[part, :])
    upper, lower = split(received)
    both = dot_t(jnp.concatenate([upper, lower], axis=0), first_recv)
    own_grad_v[...] = result + both[0:OWN, :] + both[OWN : 2 * OWN, :]
    leave(own_grad_v, own_grad)
    for copy in leaving:
        copy.wait()


def shape(*dims, kind=BF16):
    return jax.ShapeDtypeStruct(dims, kind)


VMEM = pl.BlockSpec(memory_space=pltpu.VMEM)
SMEM = pl.BlockSpec(memory_space=pltpu.SMEM)
HBM = pl.BlockSpec(memory_space=pltpu.HBM)
ANY = pl.BlockSpec(memory_space=pl.ANY)


def index(*args):
    return pl.pallas_call(
        index_body,
        in_specs=[SMEM] + [VMEM] * 14,
        out_specs=[VMEM] * 6,
        out_shape=[
            shape(LOC, D), shape(ALL, 128), shape(OWN, ALL), shape(PART, LOC), shape(OWN, D), shape(8, D, kind=F32),
        ],
        compiler_params=pltpu.CompilerParams(vmem_limit_bytes=LIMIT),
        cost_estimate=pl.CostEstimate(flops=200_000_000, bytes_accessed=3_000_000, transcendentals=0),
        name="index",
    )(*args)


def layer(*args):
    return pl.pallas_call(
        layer_body,
        in_specs=[SMEM] + [ANY] * INPUTS,
        out_specs=[ANY] * OUTPUTS,
        out_shape=[
            shape(OWN, D), shape(LOC, D), shape(CUT, D), shape(OWN, D, kind=F32),
            shape(CUT // 2, D), shape(CUT // 2, D),
            shape(PART // 2, D, kind=F32), shape(PART // 2, D),
        ],
        scratch_shapes=[
            pltpu.VMEM((X, Z, PACK, D), BF16),
            pltpu.VMEM((X, Z, PACK, D), BF16),
            pltpu.VMEM((ALL, D), BF16),
            pltpu.VMEM((ALL, D), BF16),
            pltpu.VMEM((ALL, 128), BF16),
            pltpu.VMEM((OWN, ALL), BF16),
            pltpu.VMEM((PART, LOC), BF16),
            pltpu.VMEM((OWN, D), BF16),
            pltpu.VMEM((OWN, D), BF16),
            pltpu.VMEM((8, D), F32),
            *[pltpu.VMEM((F, C, size, D), BF16) for _, size in WEIGHTS],
            pltpu.VMEM((GROUPS, GROUP, GROUP), BF16),
            pltpu.VMEM((Z * X * C, D), F32),
            pltpu.VMEM((ALL, D), F32),
            pltpu.VMEM((ALL, D), F32),
            pltpu.VMEM((ALL, 1), F32),
            pltpu.VMEM((OWN, D), BF16),
            pltpu.VMEM((OWN, D), F32),
            pltpu.VMEM((CUT // 2, D), BF16),
            pltpu.VMEM((CUT // 2, D), BF16),
            pltpu.VMEM((PART // 2, D), F32),
            pltpu.VMEM((PART // 2, D), BF16),
            pltpu.SemaphoreType.DMA((11,)),
            pltpu.SemaphoreType.DMA((4, C)),
            pltpu.SemaphoreType.DMA((17,)),
        ],
        compiler_params=pltpu.CompilerParams(vmem_limit_bytes=LIMIT),
        cost_estimate=pl.CostEstimate(flops=4_000_000_000, bytes_accessed=12_000_000, transcendentals=600_000),
        name="layer",
    )(*args)


def after_body(values, other, out):
    del values, other, out


def after(values, other):
    return pl.pallas_call(
        after_body,
        in_specs=[HBM, ANY],
        out_specs=HBM,
        out_shape=jax.ShapeDtypeStruct(values.shape, values.dtype),
        input_output_aliases={0: 0},
        compiler_params=pltpu.CompilerParams(vmem_limit_bytes=LIMIT),
        cost_estimate=pl.CostEstimate(flops=0, bytes_accessed=0, transcendentals=0),
        name="after",
    )(values, other)


def pack_body(core, first, second, third, fourth, out, half, sems):
    start = 0
    for ref in (first, second, third, fourth):
        size = ref.shape[0] // C
        half[start : start + size, :] = ref[pl.ds(pl.multiple_of(core[0] * size, 32), size), :]
        start += size
    copies = [pltpu.make_async_copy(half, out.at[f], sems.at[f]) for f in range(F)]
    for copy in copies:
        copy.start()
    for copy in copies:
        copy.wait()


def pack(core, *parts):
    rows = sum(part.shape[0] for part in parts) // C
    return pl.pallas_call(
        pack_body,
        in_specs=[SMEM] + [VMEM] * 4,
        out_specs=HBM,
        out_shape=shape(F, rows, D),
        scratch_shapes=[pltpu.VMEM((rows, D), BF16), pltpu.SemaphoreType.DMA((F,))],
        compiler_params=pltpu.CompilerParams(vmem_limit_bytes=LIMIT),
        cost_estimate=pl.CostEstimate(flops=0, bytes_accessed=2_000_000, transcendentals=0),
        name="pack",
    )(core, *parts)


def shift(values, axis, size, step):
    return lax.ppermute(values, axis, [(i, (i + step) % size) for i in range(size)])


def stage_body(values, out, sem):
    copy = pltpu.make_async_copy(values, out, sem)
    copy.start()
    copy.wait()


def stage(values):
    return pl.pallas_call(
        stage_body,
        in_specs=[ANY],
        out_specs=VMEM,
        out_shape=jax.ShapeDtypeStruct(values.shape, values.dtype),
        scratch_shapes=[pltpu.SemaphoreType.DMA],
        compiler_params=pltpu.CompilerParams(vmem_limit_bytes=8 * 1024 * 1024),
        cost_estimate=pl.CostEstimate(flops=0, bytes_accessed=1_000_000, transcendentals=0),
        name="stage",
    )(values)


def exchange(values, axis):
    return lax.all_to_all(values, axis, split_axis=0, concat_axis=0, tiled=True)


def shards(
    node_in, local_edges, cut_edges, node_cot, edge_w1, edge_w2, node_w1, node_w2,
    edge_b1, edge_b2, edge_gain, edge_shift, node_b1, node_b2, node_gain, node_shift,
    local_send, local_recv, cut_send, cut_recv, cut_count,
):
    feat = lax.axis_index("feat")
    core = lax.axis_index("core")
    weights = exchange(pack(core.astype(jnp.int32).reshape(1), edge_w1, edge_w2, node_w1, node_w2), "feat")
    selectors = cut_send[0, 0].astype(BF16).reshape(2, D)
    selectors = jnp.pad(selectors, ((0, PACK - BORDER - 2), (0, 0)))
    payload = jnp.concatenate([node_in[:BORDER], selectors], axis=0)
    payload = jnp.stack([shift(payload, "z", Z, Z - 1), payload, shift(payload, "z", Z, 1)])
    payload = jnp.concatenate([payload, shift(payload, "z", Z, 3), shift(payload[1:], "z", Z, Z - 3)], axis=0)
    near = jnp.stack([payload] + [shift(payload, "x", X, step) for step in range(1, X)])
    far = shift(near, "core", C, 1)
    owner = jnp.bitwise_xor(local_send // OWN, feat.astype(jnp.int32))
    owner = (owner & 1) * 4 + (owner & 2) + (owner >> 2)
    relative = owner * OWN + local_send % OWN
    vectors = (edge_b1, edge_b2, edge_gain, edge_shift, node_b1, node_b2, node_gain, node_shift)
    indices = index(
        feat.astype(jnp.int32).reshape(1), node_in, local_send[None, :], relative[None, :], local_recv[None, :],
        cut_recv[0], cut_count[0], *[v[None, :] for v in vectors],
    )
    place = jnp.stack([lax.axis_index(axis) for axis in DOM]).astype(jnp.int32)
    weights = after(weights, far)
    other_weights = shift(weights, "core", C, 1)
    node_out, local_grad, cut_grad, own_grad, keep, send, local_keep, local_sums = layer(
        place, weights, other_weights, near, far, local_edges, cut_edges, *indices, node_cot
    )
    summed = stage(keep).astype(F32) + lax.ppermute(send, "core", [(0, 1), (1, 0)]).astype(F32)
    for distance in (1, 2, 4):
        if distance > 1:
            half = local_keep.shape[0] // 2
            local_keep, local_sums = local_keep[:half], local_keep[half:].astype(BF16)
        arrived = lax.ppermute(local_sums, "feat", [(f, f ^ distance) for f in range(F)])
        local_keep = local_keep + arrived.astype(F32)
    summed = summed.astype(BF16)
    summed = exchange(summed.reshape(Z * X, BORDER, D), ("z", "x"))
    summed = jnp.sum(summed.astype(F32), axis=0).astype(BF16)
    summed = exchange(jnp.broadcast_to(summed[None], (F, BORDER, D)), "feat")
    summed = jnp.where(feat == 0, jnp.sum(summed.astype(F32), axis=0), 0.0)
    node_grad = own_grad + local_keep + jnp.pad(summed, ((0, OWN - BORDER), (0, 0)))
    return node_out, node_grad, local_grad, cut_grad


def solution(mesh):
    split_mesh = Mesh(mesh.devices.reshape(Z, X, C, F), (*DOM, "feat"))
    both = (*DOM, "feat")
    placed = (
        P(DOM, None),
        *[P(both, None)] * 3,
        *[P("feat", None)] * 4,
        *[P()] * 8,
        *[P(both)] * 2,
        *[P(DOM, "feat", None)] * 3,
    )
    return jax.shard_map(
        shards,
        mesh=split_mesh,
        in_specs=placed,
        out_specs=(P(both, None),) * 4,
        check_vma=False,
    )
```
